256 devices in a mesh: kz: 16 (over z_lo, x, core), freq: 16 (over z_hi, y).
Axes of the slice: x: 4, y: 4, z: 8 (z_hi: 4, z_lo: 2; z = z_hi * 2 + z_lo), core: 2. Of those that a mesh axis runs over, the one named last changes fastest.
Arguments:
- green: float32 [1, 2, 512, 32, 1024], P(None, None, 'freq', 'kz'), may hold values from -6 to 6
- interaction: float32 [1, 2, 256, 32, 1024], P(None, None, 'freq', 'kz'), may hold values from -6 to 6
Outputs:
- self_energy: float32 [2, 512, 32, 1024], P(None, 'freq', 'kz')
- bubble: float32 [1, 2, 256, 32, 1024], P(None, None, 'freq', 'kz')
The draws below stay inside these ranges and needn't reach their ends.
All inputs are finite; a program needn't handle non-finite values.
Results may differ from the reference program's by a relative error of at most 0.000098.
Values sent between devices are 32-bit elements; how exact they have to be, the bound alone decides.
A program may use at most 64 MiB of HBM per device.

```python
import math
import jax
import jax.numpy as jnp
from jax import lax

KX = 32
KY = 32
KZ = 32
NF = 512
NB = 256
NTAU = 512
GP = 1
XY = 1024


def block_levels(rng, shape, shards, low, top_value):
    level = 1.0
    for axis_at, parts in shards:
        steps = jax.random.uniform(jax.random.fold_in(jax.random.fold_in(rng, 6), axis_at), (parts,), jnp.float32, low / len(shards), top_value / len(shards))
        level = level * jnp.repeat(jnp.exp(steps), shape[axis_at] // parts).reshape((-1,) + (1,) * (len(shape) - 1 - axis_at))
    return level


def bell_draw(rng, extent, scale, reach, pieces=(), held_as=jnp.bfloat16):
    result = jax.random.normal(rng, extent, jnp.float32) * scale
    if len(pieces) > 0:
        result = block_levels(rng, extent, pieces, -0.22, 0.18) * result
    return jnp.clip(result, min=-reach, max=reach).astype(held_as)


def setup_inputs(seed: int = 0) -> dict:
    keys = jax.random.split(jax.random.key(seed), 3)
    return {
        "green": bell_draw(keys[0], (GP, 2, NF, KZ, XY), 1.0, 6.0, ((2, 16), (3, 16)), jnp.float32),
        "interaction": bell_draw(keys[1], (GP, 2, NB, KZ, XY), 1.0, 6.0, ((2, 16), (3, 16)), jnp.float32),
    }


def to_complex(field):
    return lax.complex(field[:, 0], field[:, 1])

def edge_phase(offset, length):
    positions = jnp.arange(NTAU, dtype=jnp.int32)
    windings = jnp.mod((offset - length) * (2 * positions + 1), 4 * NTAU)
    return 2.0 * math.pi * windings.astype(jnp.float32) / (4.0 * NTAU)

def forward(field, offset):
    number = field.shape[0]
    length = field.shape[1]
    grid = field.reshape(number, length, KZ, KX, KY)
    grid = jnp.fft.ifftn(grid, axes=(2, 3, 4)) * math.sqrt(KZ * KX * KY)
    positions = jnp.arange(length, dtype=jnp.int32).astype(jnp.float32)
    before = jnp.exp(-1j * (math.pi * positions / NTAU))
    grid = grid * before[None, :, None, None, None]
    grid = jnp.fft.fft(grid, n=NTAU, axis=1)
    after = jnp.exp(-1j * edge_phase(offset, length))
    return grid * after[None, :, None, None, None] / math.sqrt(length)

def backward(field, offset, length):
    number = field.shape[0]
    after = jnp.exp(1j * edge_phase(offset, length))
    grid = field * after[None, :, None, None, None]
    grid = jnp.fft.ifft(grid, axis=1) * NTAU
    grid = grid[:, :length]
    positions = jnp.arange(length, dtype=jnp.int32).astype(jnp.float32)
    before = jnp.exp(1j * (math.pi * positions / NTAU))
    grid = grid * before[None, :, None, None, None] / math.sqrt(NTAU)
    grid = jnp.fft.fftn(grid, axes=(2, 3, 4)) / math.sqrt(KZ * KX * KY)
    stacked = jnp.stack([jnp.real(grid), jnp.imag(grid)], 1)
    return stacked.reshape(number, 2, length, KZ, KX * KY).astype(jnp.float32)

def reference(green, interaction):
    green_time = forward(to_complex(green), 1)
    inter_time = forward(to_complex(interaction), 0)
    green_mirror = jnp.roll(jnp.flip(green_time, axis=(2, 3, 4)), 1, axis=(2, 3, 4))
    sigma_time = lax.optimization_barrier(jnp.sum(inter_time * green_time, axis=0, keepdims=True))
    bubble_time = -(green_time * jnp.flip(green_mirror, axis=1))
    self_energy = backward(sigma_time, 1, NF)[0]
    bubble = backward(bubble_time, 0, NB)
    return (self_energy, bubble)
```

```python
import functools
import math

import jax
import jax.numpy as jnp
import ml_dtypes
import numpy as np
from jax import lax
from jax.experimental import pallas as pl
from jax.experimental.pallas import tpu as pltpu
from jax.sharding import PartitionSpec as P

MESH = pl.DeviceIdType.MESH
F32 = jnp.float32
BF16 = jnp.bfloat16


def split_table(table):
    high = table.astype(ml_dtypes.bfloat16)
    low = (table - high.astype(np.float64)).astype(ml_dtypes.bfloat16)
    return np.stack([high, low])


def y_sets():
    sets = [[0, 16, 8, 24]]
    singles = [v for v in range(1, 16) if v != 8]
    for k in range(7):
        a, b = singles[2 * k], singles[2 * k + 1]
        sets.append([a, 32 - a, b, 32 - b])
    return sets


def columns(residue):
    if residue == 0:
        xs = [[0, 8], [16, 24]]
    elif residue == 4:
        xs = [[4, 12], [28, 20]]
    elif residue < 4:
        m = residue
        xs = [[m, m + 8], [m + 16, m + 24]]
    else:
        m = 8 - residue
        xs = [[16 - m, 8 - m], [32 - m, 24 - m]]
    sets = y_sets()
    x = np.zeros(128, np.int64)
    y = np.zeros(128, np.int64)
    for pair in range(2):
        for k in range(8):
            for half in range(2):
                for i in range(4):
                    lane = pair * 64 + k * 8 + half * 4 + i
                    x[lane] = xs[half][pair]
                    y[lane] = sets[k][i]
    return x, y


def real_form(angle, scale):
    c, s = np.cos(angle) * scale, np.sin(angle) * scale
    return np.block([[c, s], [-s, c]])


def sheet_tables():
    tables = []
    xl = np.repeat(np.arange(4), 32)
    ky = np.tile(np.arange(32), 4)
    for residue in range(8):
        x, y = columns(residue)
        angle = 2 * np.pi * ((xl[:, None] * x + ky[:, None] * y) % 32) / 32
        tables.append(real_form(angle, 1 / 32))
    return np.stack(tables)


def depth_tables():
    whole, parts = [], []
    kappa = np.arange(16)
    for parity in range(2):
        depth = 2 * np.arange(16) + parity
        angle = 2 * np.pi * ((depth[:, None] * kappa) % 32) / 32
        c, s = np.cos(angle) / math.sqrt(32), np.sin(angle) / math.sqrt(32)
        eye = np.eye(8)
        whole.append(np.block([[np.kron(c, eye), np.kron(-s, eye)], [np.kron(s, eye), np.kron(c, eye)]]))
        parts.append(np.concatenate([np.kron(c, eye), np.kron(s, eye)], 0))
    return np.stack(whole), np.stack(parts)


def angles(length, offset):
    p = 2 * np.arange(length) - length + offset
    j = np.arange(256)
    return 2 * np.pi * ((p[:, None] * (2 * j + 1)) % 2048) / 2048


def fermi_table():
    theta = angles(512, 1).reshape(4, 4, 32, 256).transpose(1, 0, 2, 3).reshape(512, 256)
    return np.concatenate([np.cos(theta), np.sin(theta)], 1) / math.sqrt(512)


def bose_tables():
    theta = angles(256, 0).reshape(4, 4, 16, 256).transpose(1, 0, 2, 3)
    c, s = np.cos(theta), np.sin(theta)
    real = np.concatenate([c, -s, c, s], -1)
    imag = np.concatenate([s, c, -s, c], -1)
    there = np.stack([real, imag], 1).reshape(512, 1024) / math.sqrt(256)
    zero = np.zeros_like(c)
    real = np.concatenate([c, zero, zero, -s], -1)
    imag = np.concatenate([zero, c, s, zero], -1)
    back = np.stack([real, imag], 1).reshape(512, 1024).T / math.sqrt(512)
    return there, back


def mirror_tables():
    tables = np.zeros((8, 128, 128))
    for parity in range(2):
        for self_x in range(2):
            for self_y in range(2):
                for depth in range(16):
                    other = (-depth - parity) % 16
                    for half in range(2):
                        for i in range(4):
                            h = half if self_x else 1 - half
                            n = [0, 1, 3, 2][i] if self_y else [1, 0, 3, 2][i]
                            row = depth * 8 + half * 4 + i
                            tables[parity * 4 + self_x * 2 + self_y, row, other * 8 + h * 4 + n] = 1
    return tables.astype(ml_dtypes.bfloat16)


@functools.cache
def tables():
    sheet = sheet_tables()
    whole, parts = depth_tables()
    fermi = fermi_table()
    there, back = bose_tables()
    parts_back = np.concatenate(
        [parts[:, :128].transpose(0, 2, 1), parts[:, 128:].transpose(0, 2, 1)], 1
    )
    return (
        split_table(sheet),
        split_table(sheet.transpose(0, 2, 1)),
        np.ascontiguousarray(split_table(whole).swapaxes(0, 1)),
        np.ascontiguousarray(split_table(whole.transpose(0, 2, 1)).swapaxes(0, 1)),
        np.ascontiguousarray(split_table(parts).swapaxes(0, 1)),
        np.ascontiguousarray(split_table(parts_back).swapaxes(0, 1)),
        split_table(fermi),
        split_table(fermi.T),
        split_table(there),
        split_table(back),
        mirror_tables(),
    )


def split(x):
    high = x.astype(BF16)
    return high, (x - high.astype(F32)).astype(BF16)


def dot(a, b):
    return jnp.dot(a, b, preferred_element_type=F32)


def data_by_table(x, table):
    high, low = split(x)
    return dot(high, table[0]) + dot(low, table[0]) + dot(high, table[1])


def table_by_data(table, x):
    high, low = split(x)
    return dot(table[0], high) + dot(table[0], low) + dot(table[1], high)


def four(re, im, sign):
    s0r, s0i = re[0] + re[2], im[0] + im[2]
    d0r, d0i = re[0] - re[2], im[0] - im[2]
    s1r, s1i = re[1] + re[3], im[1] + im[3]
    d1r, d1i = re[1] - re[3], im[1] - im[3]
    tr, ti = (-d1i, d1r) if sign > 0 else (d1i, -d1r)
    return [s0r + s1r, d0r + tr, s0r - s1r, d0r - tr], [s0i + s1i, d0i + ti, s0i - s1i, d0i - ti]


def eight(re, im, sign):
    er, ei = four(re[0::2], im[0::2], sign)
    orr, oi = four(re[1::2], im[1::2], sign)
    h = math.sqrt(0.5)
    tr = [orr[0]]
    ti = [oi[0]]
    if sign > 0:
        tr += [h * (orr[1] - oi[1]), -oi[2], -h * (orr[3] + oi[3])]
        ti += [h * (orr[1] + oi[1]), orr[2], h * (orr[3] - oi[3])]
    else:
        tr += [h * (orr[1] + oi[1]), oi[2], h * (oi[3] - orr[3])]
        ti += [h * (oi[1] - orr[1]), -orr[2], -h * (orr[3] + oi[3])]
    return (
        [er[k] + tr[k] for k in range(4)] + [er[k] - tr[k] for k in range(4)],
        [ei[k] + ti[k] for k in range(4)] + [ei[k] - ti[k] for k in range(4)],
    )


PAIRS = ((1, 7, 2), (2, 6, 4), (3, 5, 6))


def sheet_there(x, table, out):
    rows = x.shape[1]
    re = [x[0, :, 128 * g : 128 * g + 128] for g in range(8)]
    im = [x[1, :, 128 * g : 128 * g + 128] for g in range(8)]
    yr, yi = eight(re, im, 1)
    first = lax.broadcasted_iota(jnp.int32, (rows, 256), 1) % 8 < 4

    def one(residue):
        both = jnp.concatenate([yr[residue], yi[residue]], 1)
        return data_by_table(both, (table[0, residue], table[1, residue]))

    def put(group, value):
        out[group, 0] = value[:, :128]
        out[group, 1] = value[:, 128:]

    put(0, one(0))
    put(1, one(4))
    for m, n, group in PAIRS:
        a, b = one(m), one(n)
        put(group, jnp.where(first, a, b))
        put(group + 1, jnp.where(first, b, a))


def sheet_back(x, table, out):
    rows = x.shape[2]
    first = lax.broadcasted_iota(jnp.int32, (rows, 256), 1) % 8 < 4
    held = [None] * 8

    def get(group):
        return jnp.concatenate([x[group, 0], x[group, 1]], 1)

    held[0], held[4] = get(0), get(1)
    for m, n, group in PAIRS:
        a, b = get(group), get(group + 1)
        held[m] = jnp.where(first, a, b)
        held[n] = jnp.where(first, b, a)
    re, im = [], []
    for residue in range(8):
        y = data_by_table(held[residue], (table[0, residue], table[1, residue]))
        re.append(y[:, :128])
        im.append(y[:, 128:])
    re, im = eight(re, im, -1)
    for g in range(8):
        out[0, :, 128 * g : 128 * g + 128] = re[g]
        out[1, :, 128 * g : 128 * g + 128] = im[g]


def swap_parts(x, sign):
    rows = x.shape[0]
    lower = lax.broadcasted_iota(jnp.int32, (rows, 128), 1) < 64
    pieces = []
    for y in range(4):
        turned = pltpu.roll(x[:, 128 * y : 128 * y + 128], 64, 1)
        pieces.append(jnp.where(lower, -turned, turned) if sign > 0 else jnp.where(lower, turned, -turned))
    return jnp.concatenate(pieces, 1)


def kernel(
    green, inter, sheet_h, sheetb_h, whole_h, wholeb_h, parts_h, partsb_h, fermi_h, fermib_h, bose_h, boseb_h, mirror_h,
    out_g, out_v,
    x_g, x_v, sheet, sheetb, whole, wholeb, parts, partsb, fermi, fermib, bose, boseb, mirror,
    sa_g, sa_v, ra_g, ra_v, sb_g, sb_v, rb_g, rb_v, g_time,
    tb_g, tb_v, ub_g, ub_v, ta_g, ta_v, ua_g, ua_v, y_g, y_v,
    load_sem, sem,
):
    kz, freq = lax.axis_index("kz"), lax.axis_index("freq")
    z_lo, c = kz // 8, kz % 8
    z_hi, y = freq // 4, freq % 4
    z = z_hi * 2 + z_lo
    o = c * 4 + y
    parity = o // 16
    self_x = jnp.where(jnp.logical_and(z == 0, (o % 16) // 8 == 0), 1, 0)
    self_y = jnp.where(o % 8 == 0, 1, 0)

    loads = {}
    for k, (name, src, dst) in enumerate(
        [
            ("x_g", green, x_g),
            ("sheet", sheet_h, sheet),
            ("x_v", inter, x_v),
            ("whole", whole_h.at[parity], whole),
            ("fermi", fermi_h, fermi),
            ("mirror", mirror_h.at[parity * 4 + self_x * 2 + self_y], mirror),
            ("boseb", boseb_h, boseb),
            ("partsb", partsb_h.at[parity], partsb),
            ("parts", parts_h.at[parity], parts),
            ("bose", bose_h, bose),
            ("fermib", fermib_h, fermib),
            ("wholeb", wholeb_h.at[parity], wholeb),
            ("sheetb", sheetb_h, sheetb),
        ]
    ):
        loads[name] = pltpu.make_async_copy(src, dst, load_sem.at[k])
        loads[name].start()

    def z_peer(d):
        other = (z + d) % 8
        return other, {"kz": (other % 2) * 8 + c, "freq": (other // 2) * 4 + y}

    def o_peer(d):
        other = (o + d) % 32
        return other, {"kz": z_lo * 8 + other // 4, "freq": z_hi * 4 + other % 4}

    barrier = pltpu.get_barrier_semaphore()
    for d in range(1, 8):
        pl.semaphore_signal(barrier, inc=1, device_id=z_peer(d)[1], device_id_type=MESH)

    def greet(d, carry):
        pl.semaphore_signal(barrier, inc=1, device_id=o_peer(d)[1], device_id_type=MESH)
        return carry

    lax.fori_loop(1, 32, greet, 0)

    count = [0]

    def new_sem():
        count[0] += 1
        return sem.at[count[0] - 1]

    sent = []

    def exchange_z(src, dst):
        s, r, l = new_sem(), new_sem(), new_sem()
        own = pltpu.make_async_copy(src.at[z], dst.at[z], l)
        for d in (1, 7, 2, 6, 3, 5, 4):
            other, device = z_peer(d)
            pltpu.make_async_remote_copy(
                src.at[other], dst.at[z], s, r, device_id=device, device_id_type=MESH
            ).start()
        own.start()
        seven = pltpu.make_async_remote_copy(
            src.at[pl.ds(0, 7)], dst.at[pl.ds(0, 7)], s, r, device_id=z_peer(1)[1], device_id_type=MESH
        )
        sent.append(seven)

        def wait():
            seven.wait_recv()
            own.wait()

        return wait

    def exchange_o(src_at, dst_at, src_31, dst_31):
        s, r, l = new_sem(), new_sem(), new_sem()
        own = pltpu.make_async_copy(src_at(o), dst_at(o), l)

        def send(d, carry):
            other, device = o_peer(d)
            pltpu.make_async_remote_copy(
                src_at(other), dst_at(o), s, r, device_id=device, device_id_type=MESH
            ).start()
            return carry

        lax.fori_loop(1, 32, send, 0)
        own.start()
        rest = pltpu.make_async_remote_copy(
            src_31, dst_31, s, r, device_id=o_peer(1)[1], device_id_type=MESH
        )
        sent.append(rest)

        def wait():
            rest.wait_recv()
            own.wait()

        return wait

    def rows_at(ref):
        def at(k):
            piece = pl.ds(pl.multiple_of(k * 8, 8), 8)
            return ref.at[:, :, piece, :] if len(ref.shape) == 4 else ref.at[:, piece, :]

        return at

    def planes_at(ref):
        def at(k):
            planes = pl.ds(2 * (k // 4), 2)
            lanes = pl.ds(pl.multiple_of((k % 4) * 128, 128), 128)
            return ref.at[:, planes, :, lanes] if len(ref.shape) == 4 else ref.at[planes, :, lanes]

        return at

    def rows_31(ref):
        return ref.at[:, :, pl.ds(0, 248), :] if len(ref.shape) == 4 else ref.at[:, pl.ds(0, 248), :]

    loads["x_g"].wait()
    loads["sheet"].wait()
    sheet_there(x_g, sheet, sa_g)
    pl.semaphore_wait(barrier, 38)
    a_g = exchange_z(sa_g, ra_g)
    loads["x_v"].wait()
    sheet_there(x_v, sheet, sa_v)
    a_v = exchange_z(sa_v, ra_v)

    a_g()
    for p in range(2):
        for b in range(2):
            even = jnp.concatenate([ra_g[2 * h, p, pl.ds(b, 32, 2), :] for h in range(4)], 0)
            odd = jnp.concatenate([ra_g[2 * h + 1, p, pl.ds(b, 32, 2), :] for h in range(4)], 0)
            sb_g[p, b, :128, :] = (even + odd).T
            sb_g[p, b, 128:, :] = (even - odd).T
    b_g = exchange_o(rows_at(sb_g), planes_at(rb_g), rows_31(sb_g), rows_31(ub_g))
    a_v()
    for b in range(2):
        even = jnp.concatenate(
            [ra_v[2 * h, p, pl.ds(b, 16, 2), :] for p in range(2) for h in range(4)], 0
        )
        odd = jnp.concatenate(
            [ra_v[2 * h + 1, p, pl.ds(b, 16, 2), :] for p in range(2) for h in range(4)], 0
        )
        sb_v[b, :128, :] = (even + odd).T
        sb_v[b, 128:, :] = (even - odd).T
    b_v = exchange_o(rows_at(sb_v), planes_at(rb_v), rows_31(sb_v), rows_31(ub_v))

    b_g()
    loads["whole"].wait()
    lattice = table_by_data((whole[0], whole[1]), rb_g[...].reshape(256, 512))
    loads["fermi"].wait()
    both = data_by_table(lattice, (fermi[0], fermi[1]))
    ca, sa = both[:128, :256], both[:128, 256:]
    cb, sb = both[128:, :256], both[128:, 256:]
    g_time[...] = jnp.concatenate([ca + sb, cb - sa, sb - ca, -(cb + sa)], 1)
    g1r, g1i, g2r, g2i = [g_time[:, 256 * k : 256 * k + 256] for k in range(4)]
    loads["mirror"].wait()
    high, low = split(g_time[...])
    turned = dot(mirror[...], high) + dot(mirror[...], low)
    m1r, m1i, m2r, m2i = [turned[:, 256 * k : 256 * k + 256] for k in range(4)]
    b1r, b1i = g1i * m2i - g1r * m2r, -(g1r * m2i + g1i * m2r)
    b2r, b2i = g2i * m1i - g2r * m1r, -(g2r * m1i + g2i * m1r)
    loads["boseb"].wait()
    nu = data_by_table(
        jnp.concatenate([b1r + b2r, b1i + b2i, b1r - b2r, b1i - b2i], 1), (boseb[0], boseb[1])
    )
    loads["partsb"].wait()
    cs = table_by_data((partsb[0], partsb[1]), nu)
    tb_v[...] = (cs[:128] + swap_parts(cs[128:], -1)).reshape(16, 8, 512)
    c_v = exchange_o(planes_at(tb_v), rows_at(ub_v), rows_31(sb_v), rows_31(ub_v))

    b_v()
    loads["parts"].wait()
    cs = table_by_data((parts[0], parts[1]), rb_v[...].reshape(128, 512))
    loads["bose"].wait()
    v_time = data_by_table(cs[:128] + swap_parts(cs[128:], 1), (bose[0], bose[1]))
    v1r, v1i, v2r, v2i = [v_time[:, 256 * k : 256 * k + 256] for k in range(4)]
    g1r, g1i, g2r, g2i = [g_time[:, 256 * k : 256 * k + 256] for k in range(4)]
    s1r, s1i = v1r * g1r - v1i * g1i, v1r * g1i + v1i * g1r
    s2r, s2i = v2r * g2r - v2i * g2i, v2r * g2i + v2i * g2r
    loads["fermib"].wait()
    omega = data_by_table(
        jnp.concatenate(
            [
                jnp.concatenate([s1r - s2r, -(s1i + s2i)], 1),
                jnp.concatenate([s1i - s2i, s1r + s2r], 1),
            ],
            0,
        ),
        (fermib[0], fermib[1]),
    )
    loads["wholeb"].wait()
    tb_g[...] = table_by_data((wholeb[0], wholeb[1]), omega).reshape(2, 16, 8, 512)
    c_g = exchange_o(planes_at(tb_g), rows_at(ub_g), rows_31(sb_g), rows_31(ub_g))

    c_v()
    for b in range(2):
        even, odd = ub_v[b, :128, :].T, ub_v[b, 128:, :].T
        for lo, value in ((0, even + odd), (1, even - odd)):
            for p in range(2):
                for h in range(4):
                    k = 64 * p + 16 * h
                    ta_v[2 * h + lo, p, pl.ds(b, 16, 2), :] = value[k : k + 16]
    d_v = exchange_z(ta_v, ua_v)
    c_g()
    for p in range(2):
        for b in range(2):
            even, odd = ub_g[p, b, :128, :].T, ub_g[p, b, 128:, :].T
            for lo, value in ((0, even + odd), (1, even - odd)):
                for h in range(4):
                    ta_g[2 * h + lo, p, pl.ds(b, 32, 2), :] = value[32 * h : 32 * h + 32]
    d_g = exchange_z(ta_g, ua_g)

    d_v()
    loads["sheetb"].wait()
    sheet_back(ua_v, sheetb, y_v)
    put_v = pltpu.make_async_copy(y_v, out_v, load_sem.at[13])
    put_v.start()
    d_g()
    sheet_back(ua_g, sheetb, y_g)
    put_g = pltpu.make_async_copy(y_g, out_g, load_sem.at[14])
    put_g.start()
    for copy in sent:
        copy.wait_send()
    put_v.wait()
    put_g.wait()


def per_device(green, inter):
    shapes = [
        (2, 64, 1024), (2, 32, 1024),
        (2, 8, 256, 256), (2, 8, 256, 256), (2, 256, 256), (2, 256, 256), (2, 256, 128), (2, 256, 128),
        (2, 512, 512), (2, 512, 512), (2, 512, 1024), (2, 1024, 512), (128, 128),
        (8, 2, 64, 128), (8, 2, 32, 128), (8, 2, 64, 128), (8, 2, 32, 128),
        (2, 2, 256, 128), (2, 256, 128), (2, 16, 8, 512), (16, 8, 512), (128, 1024),
        (2, 16, 8, 512), (16, 8, 512), (2, 2, 256, 128), (2, 256, 128),
        (8, 2, 64, 128), (8, 2, 32, 128), (8, 2, 64, 128), (8, 2, 32, 128), (2, 64, 1024), (2, 32, 1024),
    ]
    scratch = [pltpu.VMEM(s, BF16 if 2 <= k < 13 else F32) for k, s in enumerate(shapes)]
    any_spec = pl.BlockSpec(memory_space=pl.ANY)
    constants = tables()
    out_g, out_v = pl.pallas_call(
        kernel,
        out_shape=(
            jax.ShapeDtypeStruct((2, 64, 1024), F32),
            jax.ShapeDtypeStruct((2, 32, 1024), F32),
        ),
        in_specs=[any_spec] * (2 + len(constants)),
        out_specs=(any_spec, any_spec),
        scratch_shapes=scratch + [pltpu.SemaphoreType.DMA((15,)), pltpu.SemaphoreType.DMA((24,))],
        compiler_params=pltpu.CompilerParams(
            collective_id=0, has_side_effects=True, vmem_limit_bytes=56 << 20
        ),
    )(green.reshape(2, 64, 1024), inter.reshape(2, 32, 1024), *constants)
    return out_g.reshape(2, 32, 2, 1024), out_v.reshape(1, 2, 16, 2, 1024)


def solution(mesh):
    placed = (P(None, None, "freq", "kz", None), P(None, None, "freq", "kz", None))
    return jax.shard_map(
        per_device,
        mesh=mesh,
        in_specs=placed,
        out_specs=(P(None, "freq", "kz", None), P(None, None, "freq", "kz", None)),
        check_vma=False,
    )
```

```python
import functools
import math

import jax
import jax.numpy as jnp
import ml_dtypes
import numpy as np
from jax import lax
from jax.experimental import pallas as pl
from jax.experimental.pallas import tpu as pltpu
from jax.sharding import PartitionSpec as P

MESH = pl.DeviceIdType.MESH
F32 = jnp.float32
BF16 = jnp.bfloat16


def split_table(table):
    high = table.astype(ml_dtypes.bfloat16)
    low = (table - high.astype(np.float64)).astype(ml_dtypes.bfloat16)
    return np.stack([high, low])


def y_sets():
    sets = [[0, 16, 8, 24]]
    singles = [v for v in range(1, 16) if v != 8]
    for k in range(7):
        a, b = singles[2 * k], singles[2 * k + 1]
        sets.append([a, 32 - a, b, 32 - b])
    return sets


def columns(residue):
    if residue == 0:
        xs = [[0, 8], [16, 24]]
    elif residue == 4:
        xs = [[4, 12], [28, 20]]
    elif residue < 4:
        m = residue
        xs = [[m, m + 8], [m + 16, m + 24]]
    else:
        m = 8 - residue
        xs = [[16 - m, 8 - m], [32 - m, 24 - m]]
    sets = y_sets()
    x = np.zeros(128, np.int64)
    y = np.zeros(128, np.int64)
    for pair in range(2):
        for k in range(8):
            for half in range(2):
                for i in range(4):
                    lane = pair * 64 + k * 8 + half * 4 + i
                    x[lane] = xs[half][pair]
                    y[lane] = sets[k][i]
    return x, y


def real_form(angle, scale):
    c, s = np.cos(angle) * scale, np.sin(angle) * scale
    return np.block([[c, s], [-s, c]])


def sheet_tables():
    tables = []
    xl = np.repeat(np.arange(4), 32)
    ky = np.tile(np.arange(32), 4)
    for residue in range(8):
        x, y = columns(residue)
        angle = 2 * np.pi * ((xl[:, None] * x + ky[:, None] * y) % 32) / 32
        tables.append(real_form(angle, 1 / 32))
    return np.stack(tables)


def depth_tables():
    whole, parts = [], []
    kappa = np.arange(16)
    for parity in range(2):
        depth = 2 * np.arange(16) + parity
        angle = 2 * np.pi * ((depth[:, None] * kappa) % 32) / 32
        c, s = np.cos(angle) / math.sqrt(32), np.sin(angle) / math.sqrt(32)
        eye = np.eye(8)
        whole.append(np.block([[np.kron(c, eye), np.kron(-s, eye)], [np.kron(s, eye), np.kron(c, eye)]]))
        parts.append(np.concatenate([np.kron(c, eye), np.kron(s, eye)], 0))
    return np.stack(whole), np.stack(parts)


def angles(length, offset):
    p = 2 * np.arange(length) - length + offset
    j = np.arange(256)
    return 2 * np.pi * ((p[:, None] * (2 * j + 1)) % 2048) / 2048


def fermi_table():
    theta = angles(512, 1).reshape(4, 4, 32, 256).transpose(1, 0, 2, 3).reshape(512, 256)
    return np.concatenate([np.cos(theta), np.sin(theta)], 1) / math.sqrt(512)


def bose_tables():
    theta = angles(256, 0).reshape(4, 4, 16, 256).transpose(1, 0, 2, 3)
    c, s = np.cos(theta), np.sin(theta)
    real = np.concatenate([c, -s, c, s], -1)
    imag = np.concatenate([s, c, -s, c], -1)
    there = np.stack([real, imag], 1).reshape(512, 1024) / math.sqrt(256)
    zero = np.zeros_like(c)
    real = np.concatenate([c, zero, zero, -s], -1)
    imag = np.concatenate([zero, c, s, zero], -1)
    back = np.stack([real, imag], 1).reshape(512, 1024).T / math.sqrt(512)
    return there, back


def mirror_tables():
    tables = np.zeros((8, 128, 128))
    for parity in range(2):
        for self_x in range(2):
            for self_y in range(2):
                for depth in range(16):
                    other = (-depth - parity) % 16
                    for half in range(2):
                        for i in range(4):
                            h = half if self_x else 1 - half
                            n = [0, 1, 3, 2][i] if self_y else [1, 0, 3, 2][i]
                            row = depth * 8 + half * 4 + i
                            tables[parity * 4 + self_x * 2 + self_y, row, other * 8 + h * 4 + n] = 1
    return tables.astype(ml_dtypes.bfloat16)


@functools.cache
def tables():
    sheet = sheet_tables()
    whole, parts = depth_tables()
    fermi = fermi_table()
    there, back = bose_tables()
    parts_back = np.concatenate(
        [parts[:, :128].transpose(0, 2, 1), parts[:, 128:].transpose(0, 2, 1)], 1
    )
    return (
        split_table(sheet),
        split_table(sheet.transpose(0, 2, 1)),
        np.ascontiguousarray(split_table(whole).swapaxes(0, 1)),
        np.ascontiguousarray(split_table(whole.transpose(0, 2, 1)).swapaxes(0, 1)),
        np.ascontiguousarray(split_table(parts).swapaxes(0, 1)),
        np.ascontiguousarray(split_table(parts_back).swapaxes(0, 1)),
        split_table(fermi),
        split_table(fermi.T),
        split_table(there),
        split_table(back),
        mirror_tables(),
    )


def split(x):
    high = x.astype(BF16)
    return high, (x - high.astype(F32)).astype(BF16)


def dot(a, b):
    return jnp.dot(a, b, preferred_element_type=F32)


def data_by_table(x, table):
    high, low = split(x)
    return dot(high, table[0]) + dot(low, table[0]) + dot(high, table[1])


def table_by_data(table, x):
    high, low = split(x)
    return dot(table[0], high) + dot(table[0], low) + dot(table[1], high)


def four(re, im, sign):
    s0r, s0i = re[0] + re[2], im[0] + im[2]
    d0r, d0i = re[0] - re[2], im[0] - im[2]
    s1r, s1i = re[1] + re[3], im[1] + im[3]
    d1r, d1i = re[1] - re[3], im[1] - im[3]
    tr, ti = (-d1i, d1r) if sign > 0 else (d1i, -d1r)
    return [s0r + s1r, d0r + tr, s0r - s1r, d0r - tr], [s0i + s1i, d0i + ti, s0i - s1i, d0i - ti]


def eight(re, im, sign):
    er, ei = four(re[0::2], im[0::2], sign)
    orr, oi = four(re[1::2], im[1::2], sign)
    h = math.sqrt(0.5)
    tr = [orr[0]]
    ti = [oi[0]]
    if sign > 0:
        tr += [h * (orr[1] - oi[1]), -oi[2], -h * (orr[3] + oi[3])]
        ti += [h * (orr[1] + oi[1]), orr[2], h * (orr[3] - oi[3])]
    else:
        tr += [h * (orr[1] + oi[1]), oi[2], h * (oi[3] - orr[3])]
        ti += [h * (oi[1] - orr[1]), -orr[2], -h * (orr[3] + oi[3])]
    return (
        [er[k] + tr[k] for k in range(4)] + [er[k] - tr[k] for k in range(4)],
        [ei[k] + ti[k] for k in range(4)] + [ei[k] - ti[k] for k in range(4)],
    )


PAIRS = ((1, 7, 2), (2, 6, 4), (3, 5, 6))


def sheet_there(x, plane, rows, table, out):
    re = [x[0, pl.ds(2 * g + plane, rows, 16), :] for g in range(8)]
    im = [x[1, pl.ds(2 * g + plane, rows, 16), :] for g in range(8)]
    yr, yi = eight(re, im, 1)
    first = lax.broadcasted_iota(jnp.int32, (rows, 256), 1) % 8 < 4

    def one(residue):
        both = jnp.concatenate([yr[residue], yi[residue]], 1)
        return data_by_table(both, (table[0, residue], table[1, residue]))

    def put(group, value):
        out[group, 0] = value[:, :128]
        out[group, 1] = value[:, 128:]

    put(0, one(0))
    put(1, one(4))
    for m, n, group in PAIRS:
        a, b = one(m), one(n)
        put(group, jnp.where(first, a, b))
        put(group + 1, jnp.where(first, b, a))


def sheet_back(x, plane, rows, table, out):
    first = lax.broadcasted_iota(jnp.int32, (rows, 256), 1) % 8 < 4
    held = [None] * 8

    def get(group):
        return jnp.concatenate([x[group, 0], x[group, 1]], 1)

    held[0], held[4] = get(0), get(1)
    for m, n, group in PAIRS:
        a, b = get(group), get(group + 1)
        held[m] = jnp.where(first, a, b)
        held[n] = jnp.where(first, b, a)
    re, im = [], []
    for residue in range(8):
        y = data_by_table(held[residue], (table[0, residue], table[1, residue]))
        re.append(y[:, :128])
        im.append(y[:, 128:])
    re, im = eight(re, im, -1)
    for g in range(8):
        out[0, pl.ds(2 * g + plane, rows, 16), :] = re[g]
        out[1, pl.ds(2 * g + plane, rows, 16), :] = im[g]


def swap_parts(x, sign):
    rows = x.shape[0]
    lower = lax.broadcasted_iota(jnp.int32, (rows, 128), 1) < 64
    pieces = []
    for y in range(4):
        turned = pltpu.roll(x[:, 128 * y : 128 * y + 128], 64, 1)
        pieces.append(jnp.where(lower, -turned, turned) if sign > 0 else jnp.where(lower, turned, -turned))
    return jnp.concatenate(pieces, 1)


def kernel(
    green, inter, sheet_h, sheetb_h, whole_h, wholeb_h, parts_h, partsb_h, fermi_h, fermib_h, bose_h, boseb_h, mirror_h,
    out_g, out_v,
    x_g, x_v, sheet, sheetb, whole, wholeb, parts, partsb, fermi, fermib, bose, boseb, mirror,
    sa_g, sa_v, ra_g, ra_v, sb_g, sb_v, rb_g, rb_v, g_time,
    tb_g, tb_v, ub_g, ub_v, ta_g, ta_v, ua_g, ua_v, y_g, y_v,
    load_sem, sem,
):
    kz, freq = lax.axis_index("kz"), lax.axis_index("freq")
    z_lo, c = kz // 8, kz % 8
    z_hi, y = freq // 4, freq % 4
    z = z_hi * 2 + z_lo
    o = c * 4 + y
    parity = o // 16
    self_x = jnp.where(jnp.logical_and(z == 0, (o % 16) // 8 == 0), 1, 0)
    self_y = jnp.where(o % 8 == 0, 1, 0)

    loads = {}

    def load(name, src, dst):
        loads[name] = pltpu.make_async_copy(src, dst, load_sem.at[len(loads)])
        loads[name].start()

    load("x_g", green, x_g)
    load("sheet", sheet_h, sheet)
    load("x_v", inter, x_v)

    def z_peer(d):
        other = (z + d) % 8
        return other, {"kz": (other % 2) * 8 + c, "freq": (other // 2) * 4 + y}

    def o_peer(d):
        other = (o + d) % 32
        return other, {"kz": z_lo * 8 + other // 4, "freq": z_hi * 4 + other % 4}

    barrier = pltpu.get_barrier_semaphore()
    for d in range(1, 8):
        pl.semaphore_signal(barrier, inc=1, device_id=z_peer(d)[1], device_id_type=MESH)

    def greet(d, carry):
        pl.semaphore_signal(barrier, inc=1, device_id=o_peer(d)[1], device_id_type=MESH)
        return carry

    lax.fori_loop(1, 32, greet, 0)

    count = [0]

    def new_sem():
        count[0] += 1
        return sem.at[count[0] - 1]

    sent = []

    def exchange_z(src, dst):
        s, r, l = new_sem(), new_sem(), new_sem()
        own = pltpu.make_async_copy(src.at[z], dst.at[z], l)
        for d in (1, 7, 2, 6, 3, 5, 4):
            other, device = z_peer(d)
            pltpu.make_async_remote_copy(
                src.at[other], dst.at[z], s, r, device_id=device, device_id_type=MESH
            ).start()
        own.start()
        seven = pltpu.make_async_remote_copy(
            src.at[pl.ds(0, 7)], dst.at[pl.ds(0, 7)], s, r, device_id=z_peer(1)[1], device_id_type=MESH
        )
        sent.append(seven)

        def wait():
            seven.wait_recv()
            own.wait()

        return wait

    def exchange_o(src_at, dst_at, some):
        s, r, l = new_sem(), new_sem(), new_sem()
        own = pltpu.make_async_copy(src_at(o), dst_at(o), l)

        def send(d, carry):
            other, device = o_peer(d)
            pltpu.make_async_remote_copy(
                src_at(other), dst_at(o), s, r, device_id=device, device_id_type=MESH
            ).start()
            return carry

        lax.fori_loop(1, 32, send, 0)
        own.start()
        rest = pltpu.make_async_remote_copy(
            some, some, s, r, device_id=o_peer(1)[1], device_id_type=MESH
        )
        sent.append(rest)

        def wait():
            rest.wait_recv()
            own.wait()

        return wait

    def rows_g(ref, b):
        return lambda k: ref.at[b, :, pl.ds(pl.multiple_of(k * 8, 8), 8), :]

    def rows_v(ref, b):
        return lambda k: ref.at[b, pl.ds(pl.multiple_of(k * 8, 8), 8), :]

    def planes_g(ref, b):
        return lambda k: ref.at[:, 2 * (k // 4) + b, :, pl.ds(pl.multiple_of((k % 4) * 128, 128), 128)]

    def planes_v(ref, b):
        return lambda k: ref.at[2 * (k // 4) + b, :, pl.ds(pl.multiple_of((k % 4) * 128, 128), 128)]

    def some_g(ref, b):
        return ref.at[b, :, pl.ds(0, 248), :]

    def some_v(ref, b):
        return ref.at[b, pl.ds(0, 248), :]

    loads["x_g"].wait()
    loads["sheet"].wait()
    a_g, a_v, b_g, b_v, c_g, c_v, d_g, d_v = [[None, None] for _ in range(8)]
    for b in range(2):
        sheet_there(x_g, b, 32, sheet, sa_g.at[b])
        if b == 0:
            pl.semaphore_wait(barrier, 38)
        a_g[b] = exchange_z(sa_g.at[b], ra_g.at[b])
    loads["x_v"].wait()
    for b in range(2):
        sheet_there(x_v, b, 16, sheet, sa_v.at[b])
        a_v[b] = exchange_z(sa_v.at[b], ra_v.at[b])

    load("whole", whole_h.at[parity], whole)
    load("fermi", fermi_h, fermi)
    load("mirror", mirror_h.at[parity * 4 + self_x * 2 + self_y], mirror)
    load("boseb", boseb_h, boseb)
    load("partsb", partsb_h.at[parity], partsb)
    load("parts", parts_h.at[parity], parts)
    load("bose", bose_h, bose)
    load("fermib", fermib_h, fermib)
    load("wholeb", wholeb_h.at[parity], wholeb)
    load("sheetb", sheetb_h, sheetb)

    for b in range(2):
        a_g[b]()
        for p in range(2):
            even = jnp.concatenate([ra_g[b, 2 * h, p] for h in range(4)], 0)
            odd = jnp.concatenate([ra_g[b, 2 * h + 1, p] for h in range(4)], 0)
            sb_g[b, p, :128, :] = (even + odd).T
            sb_g[b, p, 128:, :] = (even - odd).T
        b_g[b] = exchange_o(rows_g(sb_g, b), planes_g(rb_g, b), some_g(ub_g, b))
    for b in range(2):
        a_v[b]()
        even = jnp.concatenate([ra_v[b, 2 * h, p] for p in range(2) for h in range(4)], 0)
        odd = jnp.concatenate([ra_v[b, 2 * h + 1, p] for p in range(2) for h in range(4)], 0)
        sb_v[b, :128, :] = (even + odd).T
        sb_v[b, 128:, :] = (even - odd).T
        b_v[b] = exchange_o(rows_v(sb_v, b), planes_v(rb_v, b), some_v(ub_v, b))

    b_g[0]()
    b_g[1]()
    loads["whole"].wait()
    lattice = table_by_data((whole[0], whole[1]), rb_g[...].reshape(256, 512))
    loads["fermi"].wait()
    both = data_by_table(lattice, (fermi[0], fermi[1]))
    ca, sa = both[:128, :256], both[:128, 256:]
    cb, sb = both[128:, :256], both[128:, 256:]
    g_time[...] = jnp.concatenate([ca + sb, cb - sa, sb - ca, -(cb + sa)], 1)
    g1r, g1i, g2r, g2i = [g_time[:, 256 * k : 256 * k + 256] for k in range(4)]
    loads["mirror"].wait()
    high, low = split(g_time[...])
    turned = dot(mirror[...], high) + dot(mirror[...], low)
    m1r, m1i, m2r, m2i = [turned[:, 256 * k : 256 * k + 256] for k in range(4)]
    b1r, b1i = g1i * m2i - g1r * m2r, -(g1r * m2i + g1i * m2r)
    b2r, b2i = g2i * m1i - g2r * m1r, -(g2r * m1i + g2i * m1r)
    loads["boseb"].wait()
    nu = data_by_table(
        jnp.concatenate([b1r + b2r, b1i + b2i, b1r - b2r, b1i - b2i], 1), (boseb[0], boseb[1])
    )
    loads["partsb"].wait()
    cs = table_by_data((partsb[0], partsb[1]), nu)
    tb_v[...] = (cs[:128] + swap_parts(cs[128:], -1)).reshape(16, 8, 512)
    for b in range(2):
        c_v[b] = exchange_o(planes_v(tb_v, b), rows_v(ub_v, b), some_v(ub_v, b))

    b_v[0]()
    b_v[1]()
    loads["parts"].wait()
    cs = table_by_data((parts[0], parts[1]), rb_v[...].reshape(128, 512))
    loads["bose"].wait()
    v_time = data_by_table(cs[:128] + swap_parts(cs[128:], 1), (bose[0], bose[1]))
    v1r, v1i, v2r, v2i = [v_time[:, 256 * k : 256 * k + 256] for k in range(4)]
    g1r, g1i, g2r, g2i = [g_time[:, 256 * k : 256 * k + 256] for k in range(4)]
    s1r, s1i = v1r * g1r - v1i * g1i, v1r * g1i + v1i * g1r
    s2r, s2i = v2r * g2r - v2i * g2i, v2r * g2i + v2i * g2r
    loads["fermib"].wait()
    omega = data_by_table(
        jnp.concatenate(
            [
                jnp.concatenate([s1r - s2r, -(s1i + s2i)], 1),
                jnp.concatenate([s1i - s2i, s1r + s2r], 1),
            ],
            0,
        ),
        (fermib[0], fermib[1]),
    )
    loads["wholeb"].wait()
    tb_g[...] = table_by_data((wholeb[0], wholeb[1]), omega).reshape(2, 16, 8, 512)
    for b in range(2):
        c_g[b] = exchange_o(planes_g(tb_g, b), rows_g(ub_g, b), some_g(ub_g, b))

    for b in range(2):
        c_v[b]()
        even, odd = ub_v[b, :128, :].T, ub_v[b, 128:, :].T
        for lo, value in ((0, even + odd), (1, even - odd)):
            for p in range(2):
                for h in range(4):
                    k = 64 * p + 16 * h
                    ta_v[b, 2 * h + lo, p] = value[k : k + 16]
        d_v[b] = exchange_z(ta_v.at[b], ua_v.at[b])
    for b in range(2):
        c_g[b]()
        for p in range(2):
            even, odd = ub_g[b, p, :128, :].T, ub_g[b, p, 128:, :].T
            for lo, value in ((0, even + odd), (1, even - odd)):
                for h in range(4):
                    ta_g[b, 2 * h + lo, p] = value[32 * h : 32 * h + 32]
        d_g[b] = exchange_z(ta_g.at[b], ua_g.at[b])

    loads["sheetb"].wait()
    for b in range(2):
        d_v[b]()
        sheet_back(ua_v.at[b], b, 16, sheetb, y_v)
    put_v = pltpu.make_async_copy(y_v, out_v, load_sem.at[13])
    put_v.start()
    for b in range(2):
        d_g[b]()
        sheet_back(ua_g.at[b], b, 32, sheetb, y_g)
    put_g = pltpu.make_async_copy(y_g, out_g, load_sem.at[14])
    put_g.start()
    for copy in sent:
        copy.wait_send()
    put_v.wait()
    put_g.wait()


def view(x):
    n = x.shape[-3]
    return x.reshape(2, n, 2, 8, 128).transpose(0, 1, 3, 2, 4).reshape(2, n * 16, 128)


def unview(x):
    n = x.shape[1] // 16
    return x.reshape(2, n, 8, 2, 128).transpose(0, 1, 3, 2, 4).reshape(2, n, 2, 1024)


def per_device(green, inter):
    shapes = [
        (2, 512, 128), (2, 256, 128),
        (2, 8, 256, 256), (2, 8, 256, 256), (2, 256, 256), (2, 256, 256), (2, 256, 128), (2, 256, 128),
        (2, 512, 512), (2, 512, 512), (2, 512, 1024), (2, 1024, 512), (128, 128),
        (2, 8, 2, 32, 128), (2, 8, 2, 16, 128), (2, 8, 2, 32, 128), (2, 8, 2, 16, 128),
        (2, 2, 256, 128), (2, 256, 128), (2, 16, 8, 512), (16, 8, 512), (128, 1024),
        (2, 16, 8, 512), (16, 8, 512), (2, 2, 256, 128), (2, 256, 128),
        (2, 8, 2, 32, 128), (2, 8, 2, 16, 128), (2, 8, 2, 32, 128), (2, 8, 2, 16, 128), (2, 512, 128), (2, 256, 128),
    ]
    scratch = [pltpu.VMEM(s, BF16 if 2 <= k < 13 else F32) for k, s in enumerate(shapes)]
    any_spec = pl.BlockSpec(memory_space=pl.ANY)
    constants = tables()
    out_g, out_v = pl.pallas_call(
        kernel,
        out_shape=(
            jax.ShapeDtypeStruct((2, 512, 128), F32),
            jax.ShapeDtypeStruct((2, 256, 128), F32),
        ),
        in_specs=[any_spec] * (2 + len(constants)),
        out_specs=(any_spec, any_spec),
        scratch_shapes=scratch + [pltpu.SemaphoreType.DMA((15,)), pltpu.SemaphoreType.DMA((48,))],
        compiler_params=pltpu.CompilerParams(
            collective_id=0, has_side_effects=True, vmem_limit_bytes=56 << 20
        ),
    )(view(green), view(inter), *constants)
    return unview(out_g), unview(out_v)[None]


def solution(mesh):
    placed = (P(None, None, "freq", "kz", None), P(None, None, "freq", "kz", None))
    return jax.shard_map(
        per_device,
        mesh=mesh,
        in_specs=placed,
        out_specs=(P(None, "freq", "kz", None), P(None, None, "freq", "kz", None)),
        check_vma=False,
    )
```

```python
import functools
import math

import jax
import jax.numpy as jnp
import ml_dtypes
import numpy as np
from jax import lax
from jax.experimental import pallas as pl
from jax.experimental.pallas import tpu as pltpu
from jax.sharding import PartitionSpec as P

MESH = pl.DeviceIdType.MESH
F32 = jnp.float32
BF16 = jnp.bfloat16


def split_table(table):
    high = table.astype(ml_dtypes.bfloat16)
    low = (table - high.astype(np.float64)).astype(ml_dtypes.bfloat16)
    return np.stack([high, low])


def y_sets():
    sets = [[0, 16, 8, 24]]
    singles = [v for v in range(1, 16) if v != 8]
    for k in range(7):
        a, b = singles[2 * k], singles[2 * k + 1]
        sets.append([a, 32 - a, b, 32 - b])
    return sets


def columns(residue):
    if residue == 0:
        xs = [[0, 8], [16, 24]]
    elif residue == 4:
        xs = [[4, 12], [28, 20]]
    elif residue < 4:
        m = residue
        xs = [[m, m + 8], [m + 16, m + 24]]
    else:
        m = 8 - residue
        xs = [[16 - m, 8 - m], [32 - m, 24 - m]]
    sets = y_sets()
    x = np.zeros(128, np.int64)
    y = np.zeros(128, np.int64)
    for pair in range(2):
        for k in range(8):
            for half in range(2):
                for i in range(4):
                    lane = pair * 64 + k * 8 + half * 4 + i
                    x[lane] = xs[half][pair]
                    y[lane] = sets[k][i]
    return x, y


def real_form(angle, scale):
    c, s = np.cos(angle) * scale, np.sin(angle) * scale
    return np.block([[c, s], [-s, c]])


def sheet_tables():
    tables = []
    xl = np.repeat(np.arange(4), 32)
    ky = np.tile(np.arange(32), 4)
    for residue in range(8):
        x, y = columns(residue)
        angle = 2 * np.pi * ((xl[:, None] * x + ky[:, None] * y) % 32) / 32
        tables.append(real_form(angle, 1 / 32))
    return np.stack(tables)


def depth_tables():
    whole, parts = [], []
    kappa = np.arange(16)
    for parity in range(2):
        depth = 2 * np.arange(16) + parity
        angle = 2 * np.pi * ((depth[:, None] * kappa) % 32) / 32
        c, s = np.cos(angle) / math.sqrt(32), np.sin(angle) / math.sqrt(32)
        eye = np.eye(8)
        whole.append(np.block([[np.kron(c, eye), np.kron(-s, eye)], [np.kron(s, eye), np.kron(c, eye)]]))
        parts.append(np.concatenate([np.kron(c, eye), np.kron(s, eye)], 0))
    return np.stack(whole), np.stack(parts)


def angles(length, offset):
    p = 2 * np.arange(length) - length + offset
    j = np.arange(256)
    return 2 * np.pi * ((p[:, None] * (2 * j + 1)) % 2048) / 2048


def fermi_table():
    theta = angles(512, 1).reshape(4, 4, 32, 256).transpose(1, 0, 2, 3).reshape(512, 256)
    return np.concatenate([np.cos(theta), np.sin(theta)], 1) / math.sqrt(512)


def bose_tables():
    theta = angles(256, 0).reshape(4, 4, 16, 256).transpose(1, 0, 2, 3)
    c, s = np.cos(theta), np.sin(theta)
    real = np.concatenate([c, -s, c, s], -1)
    imag = np.concatenate([s, c, -s, c], -1)
    there = np.stack([real, imag], 1).reshape(512, 1024) / math.sqrt(256)
    zero = np.zeros_like(c)
    real = np.concatenate([c, zero, zero, -s], -1)
    imag = np.concatenate([zero, c, s, zero], -1)
    back = np.stack([real, imag], 1).reshape(512, 1024).T / math.sqrt(512)
    return there, back


def mirror_tables():
    tables = np.zeros((8, 128, 128))
    for parity in range(2):
        for self_x in range(2):
            for self_y in range(2):
                for depth in range(16):
                    other = (-depth - parity) % 16
                    for half in range(2):
                        for i in range(4):
                            h = half if self_x else 1 - half
                            n = [0, 1, 3, 2][i] if self_y else [1, 0, 3, 2][i]
                            row = depth * 8 + half * 4 + i
                            tables[parity * 4 + self_x * 2 + self_y, row, other * 8 + h * 4 + n] = 1
    return tables.astype(ml_dtypes.bfloat16)


@functools.cache
def tables():
    sheet = sheet_tables()
    whole, parts = depth_tables()
    fermi = fermi_table()
    there, back = bose_tables()
    parts_back = np.concatenate(
        [parts[:, :128].transpose(0, 2, 1), parts[:, 128:].transpose(0, 2, 1)], 1
    )
    return (
        np.ascontiguousarray(split_table(sheet).swapaxes(0, 1)),
        np.ascontiguousarray(split_table(sheet.transpose(0, 2, 1)).swapaxes(0, 1)),
        np.ascontiguousarray(split_table(whole).swapaxes(0, 1)),
        np.ascontiguousarray(split_table(whole.transpose(0, 2, 1)).swapaxes(0, 1)),
        np.ascontiguousarray(split_table(parts).swapaxes(0, 1)),
        np.ascontiguousarray(split_table(parts_back).swapaxes(0, 1)),
        split_table(fermi),
        split_table(fermi.T),
        split_table(there),
        split_table(back),
        mirror_tables(),
    )


def split(x):
    high = x.astype(BF16)
    return high, (x - high.astype(F32)).astype(BF16)


def dot(a, b):
    return jnp.dot(a, b, preferred_element_type=F32)


def data_by_table(x, table):
    high, low = split(x)
    return dot(high, table[0]) + dot(low, table[0]) + dot(high, table[1])


def table_by_data(table, x):
    high, low = split(x)
    return dot(table[0], high) + dot(table[0], low) + dot(table[1], high)


def four(re, im, sign):
    s0r, s0i = re[0] + re[2], im[0] + im[2]
    d0r, d0i = re[0] - re[2], im[0] - im[2]
    s1r, s1i = re[1] + re[3], im[1] + im[3]
    d1r, d1i = re[1] - re[3], im[1] - im[3]
    tr, ti = (-d1i, d1r) if sign > 0 else (d1i, -d1r)
    return [s0r + s1r, d0r + tr, s0r - s1r, d0r - tr], [s0i + s1i, d0i + ti, s0i - s1i, d0i - ti]


def eight(re, im, sign):
    er, ei = four(re[0::2], im[0::2], sign)
    orr, oi = four(re[1::2], im[1::2], sign)
    h = math.sqrt(0.5)
    tr = [orr[0]]
    ti = [oi[0]]
    if sign > 0:
        tr += [h * (orr[1] - oi[1]), -oi[2], -h * (orr[3] + oi[3])]
        ti += [h * (orr[1] + oi[1]), orr[2], h * (orr[3] - oi[3])]
    else:
        tr += [h * (orr[1] + oi[1]), oi[2], h * (oi[3] - orr[3])]
        ti += [h * (oi[1] - orr[1]), -orr[2], -h * (orr[3] + oi[3])]
    return (
        [er[k] + tr[k] for k in range(4)] + [er[k] - tr[k] for k in range(4)],
        [ei[k] + ti[k] for k in range(4)] + [ei[k] - ti[k] for k in range(4)],
    )


FAR_FIRST = sorted(
    [(dx, dy, dc) for dx in range(4) for dy in range(4) for dc in range(2) if dx + dy + dc],
    key=lambda t: -(10 * min(t[0], 4 - t[0]) + 10 * min(t[1], 4 - t[1]) + t[2]),
)
ORDER = (0, 4, 1, 7, 2, 6, 3, 5)
PAIRS = ((1, 7, 2), (2, 6, 4), (3, 5, 6))


def sheet_there(x, plane, rows, table, out, loads=None):
    re = [x[0, pl.ds(2 * g + plane, rows, 16), :] for g in range(8)]
    im = [x[1, pl.ds(2 * g + plane, rows, 16), :] for g in range(8)]
    yr, yi = eight(re, im, 1)
    first = lax.broadcasted_iota(jnp.int32, (rows, 256), 1) % 8 < 4

    def one(residue):
        if loads is not None:
            loads["sheet" + str(residue)].wait()
        both = jnp.concatenate([yr[residue], yi[residue]], 1)
        return data_by_table(both, (table[residue, 0], table[residue, 1]))

    def put(group, value):
        out[group, 0] = value[:, :128]
        out[group, 1] = value[:, 128:]

    put(0, one(0))
    put(1, one(4))
    for m, n, group in PAIRS:
        a, b = one(m), one(n)
        put(group, jnp.where(first, a, b))
        put(group + 1, jnp.where(first, b, a))


def sheet_back(x, plane, rows, table, out):
    first = lax.broadcasted_iota(jnp.int32, (rows, 256), 1) % 8 < 4
    held = [None] * 8

    def get(group):
        return jnp.concatenate([x[group, 0], x[group, 1]], 1)

    held[0], held[4] = get(0), get(1)
    for m, n, group in PAIRS:
        a, b = get(group), get(group + 1)
        held[m] = jnp.where(first, a, b)
        held[n] = jnp.where(first, b, a)
    re, im = [], []
    for residue in range(8):
        y = data_by_table(held[residue], (table[residue, 0], table[residue, 1]))
        re.append(y[:, :128])
        im.append(y[:, 128:])
    re, im = eight(re, im, -1)
    for g in range(8):
        out[0, pl.ds(2 * g + plane, rows, 16), :] = re[g]
        out[1, pl.ds(2 * g + plane, rows, 16), :] = im[g]


def swap_parts(x, sign):
    rows = x.shape[0]
    lower = lax.broadcasted_iota(jnp.int32, (rows, 128), 1) < 64
    pieces = []
    for y in range(4):
        turned = pltpu.roll(x[:, 128 * y : 128 * y + 128], 64, 1)
        pieces.append(jnp.where(lower, -turned, turned) if sign > 0 else jnp.where(lower, turned, -turned))
    return jnp.concatenate(pieces, 1)


def kernel(
    green, inter, sheet_h, sheetb_h, whole_h, wholeb_h, parts_h, partsb_h, fermi_h, fermib_h, bose_h, boseb_h, mirror_h,
    out_g, out_v,
    x_g, x_v, sheet, sheetb, whole, wholeb, parts, partsb, fermi, fermib, bose, boseb, mirror,
    sa_g, sa_v, ra_g, ra_v, sb_g, sb_v, rb_g, rb_v, g_time,
    tb_g, tb_v, ub_g, ub_v, ta_g, ta_v, ua_g, ua_v, y_g, y_v,
    load_sem, sem,
):
    kz, freq = lax.axis_index("kz"), lax.axis_index("freq")
    z_lo, c = kz // 8, kz % 8
    z_hi, y = freq // 4, freq % 4
    z = z_hi * 2 + z_lo
    o = c * 4 + y
    parity = o // 16
    self_x = jnp.where(jnp.logical_and(z == 0, (o % 16) // 8 == 0), 1, 0)
    self_y = jnp.where(o % 8 == 0, 1, 0)

    loads = {}

    def load(name, src, dst):
        loads[name] = pltpu.make_async_copy(src, dst, load_sem.at[len(loads)])
        loads[name].start()

    for p in range(2):
        load("x_g" + str(p), green.at[p], x_g.at[p])
    for residue in ORDER:
        load("sheet" + str(residue), sheet_h.at[residue], sheet.at[residue])
    load("x_v", inter, x_v)

    def z_peer(d):
        other = (z + d) % 8
        return other, {"kz": (other % 2) * 8 + c, "freq": (other // 2) * 4 + y}

    def o_peer(d):
        other = (o + d) % 32
        return other, {"kz": z_lo * 8 + other // 4, "freq": z_hi * 4 + other % 4}

    def near(dx, dy, dc):
        c2 = ((c // 2 + dx) % 4) * 2 + (c + dc) % 2
        y2 = (y + dy) % 4
        return c2 * 4 + y2, {"kz": z_lo * 8 + c2, "freq": z_hi * 4 + y2}

    barrier = pltpu.get_barrier_semaphore()
    for d in range(1, 8):
        pl.semaphore_signal(barrier, inc=1, device_id=z_peer(d)[1], device_id_type=MESH)

    def greet(d, carry):
        pl.semaphore_signal(barrier, inc=1, device_id=o_peer(d)[1], device_id_type=MESH)
        return carry

    lax.fori_loop(1, 32, greet, 0)

    count = [0]

    def new_sem():
        count[0] += 1
        return sem.at[count[0] - 1]

    sent = []

    def exchange_z(src, dst):
        s, r, l = new_sem(), new_sem(), new_sem()
        own = pltpu.make_async_copy(src.at[z], dst.at[z], l)
        for d in (4, 3, 5, 2, 6, 1, 7):
            other, device = z_peer(d)
            pltpu.make_async_remote_copy(
                src.at[other], dst.at[z], s, r, device_id=device, device_id_type=MESH
            ).start()
        own.start()
        seven = pltpu.make_async_remote_copy(
            src.at[pl.ds(0, 7)], dst.at[pl.ds(0, 7)], s, r, device_id=z_peer(1)[1], device_id_type=MESH
        )
        sent.append(seven)

        def wait():
            seven.wait_recv()
            own.wait()

        return wait

    def exchange_o(src_at, dst_at, some):
        s, r, l = new_sem(), new_sem(), new_sem()
        own = pltpu.make_async_copy(src_at(o), dst_at(o), l)

        for dx, dy, dc in FAR_FIRST:
            other, device = near(dx, dy, dc)
            pltpu.make_async_remote_copy(
                src_at(other), dst_at(o), s, r, device_id=device, device_id_type=MESH
            ).start()
        own.start()
        rest = pltpu.make_async_remote_copy(
            some, some, s, r, device_id=o_peer(1)[1], device_id_type=MESH
        )
        sent.append(rest)

        def wait():
            rest.wait_recv()
            own.wait()

        return wait

    def rows_g(ref, b):
        return lambda k: ref.at[b, :, pl.ds(pl.multiple_of(k * 8, 8), 8), :]

    def rows_v(ref, b):
        return lambda k: ref.at[b, pl.ds(pl.multiple_of(k * 8, 8), 8), :]

    def planes_g(ref, b):
        return lambda k: ref.at[:, 2 * (k // 4) + b, :, pl.ds(pl.multiple_of((k % 4) * 128, 128), 128)]

    def planes_v(ref, b):
        return lambda k: ref.at[2 * (k // 4) + b, :, pl.ds(pl.multiple_of((k % 4) * 128, 128), 128)]

    def some_g(ref, b):
        return ref.at[b, :, pl.ds(0, 248), :]

    def some_v(ref, b):
        return ref.at[b, pl.ds(0, 248), :]

    loads["x_g0"].wait()
    loads["x_g1"].wait()
    a_g, a_v, b_g, b_v, c_g, c_v, d_g, d_v = [[None, None] for _ in range(8)]
    for b in range(2):
        sheet_there(x_g, b, 32, sheet, sa_g.at[b], loads if b == 0 else None)
        if b == 0:
            pl.semaphore_wait(barrier, 38)
        a_g[b] = exchange_z(sa_g.at[b], ra_g.at[b])
    loads["x_v"].wait()
    for b in range(2):
        sheet_there(x_v, b, 16, sheet, sa_v.at[b])
        a_v[b] = exchange_z(sa_v.at[b], ra_v.at[b])

    load("whole", whole_h.at[parity], whole)
    load("fermi", fermi_h, fermi)
    load("mirror", mirror_h.at[parity * 4 + self_x * 2 + self_y], mirror)
    load("boseb", boseb_h, boseb)
    load("partsb", partsb_h.at[parity], partsb)
    load("parts", parts_h.at[parity], parts)
    load("bose", bose_h, bose)
    load("fermib", fermib_h, fermib)
    load("wholeb", wholeb_h.at[parity], wholeb)
    load("sheetb", sheetb_h, sheetb)

    for b in range(2):
        a_g[b]()
        for p in range(2):
            even = jnp.concatenate([ra_g[b, 2 * h, p] for h in range(4)], 0)
            odd = jnp.concatenate([ra_g[b, 2 * h + 1, p] for h in range(4)], 0)
            sb_g[b, p, :128, :] = (even + odd).T
            sb_g[b, p, 128:, :] = (even - odd).T
        b_g[b] = exchange_o(rows_g(sb_g, b), planes_g(rb_g, b), some_g(ub_g, b))
    for b in range(2):
        a_v[b]()
        even = jnp.concatenate([ra_v[b, 2 * h, p] for p in range(2) for h in range(4)], 0)
        odd = jnp.concatenate([ra_v[b, 2 * h + 1, p] for p in range(2) for h in range(4)], 0)
        sb_v[b, :128, :] = (even + odd).T
        sb_v[b, 128:, :] = (even - odd).T
        b_v[b] = exchange_o(rows_v(sb_v, b), planes_v(rb_v, b), some_v(ub_v, b))

    b_g[0]()
    b_g[1]()
    loads["whole"].wait()
    lattice = table_by_data((whole[0], whole[1]), rb_g[...].reshape(256, 512))
    loads["fermi"].wait()
    both = data_by_table(lattice, (fermi[0], fermi[1]))
    ca, sa = both[:128, :256], both[:128, 256:]
    cb, sb = both[128:, :256], both[128:, 256:]
    g_time[...] = jnp.concatenate([ca + sb, cb - sa, sb - ca, -(cb + sa)], 1)
    g1r, g1i, g2r, g2i = [g_time[:, 256 * k : 256 * k + 256] for k in range(4)]
    loads["mirror"].wait()
    high, low = split(g_time[...])
    turned = dot(mirror[...], high) + dot(mirror[...], low)
    m1r, m1i, m2r, m2i = [turned[:, 256 * k : 256 * k + 256] for k in range(4)]
    b1r, b1i = g1i * m2i - g1r * m2r, -(g1r * m2i + g1i * m2r)
    b2r, b2i = g2i * m1i - g2r * m1r, -(g2r * m1i + g2i * m1r)
    loads["boseb"].wait()
    nu = data_by_table(
        jnp.concatenate([b1r + b2r, b1i + b2i, b1r - b2r, b1i - b2i], 1), (boseb[0], boseb[1])
    )
    loads["partsb"].wait()
    cs = table_by_data((partsb[0], partsb[1]), nu)
    tb_v[...] = (cs[:128] + swap_parts(cs[128:], -1)).reshape(16, 8, 512)
    for b in range(2):
        c_v[b] = exchange_o(planes_v(tb_v, b), rows_v(ub_v, b), some_v(ub_v, b))

    b_v[0]()
    b_v[1]()
    loads["parts"].wait()
    cs = table_by_data((parts[0], parts[1]), rb_v[...].reshape(128, 512))
    loads["bose"].wait()
    v_time = data_by_table(cs[:128] + swap_parts(cs[128:], 1), (bose[0], bose[1]))
    v1r, v1i, v2r, v2i = [v_time[:, 256 * k : 256 * k + 256] for k in range(4)]
    g1r, g1i, g2r, g2i = [g_time[:, 256 * k : 256 * k + 256] for k in range(4)]
    s1r, s1i = v1r * g1r - v1i * g1i, v1r * g1i + v1i * g1r
    s2r, s2i = v2r * g2r - v2i * g2i, v2r * g2i + v2i * g2r
    loads["fermib"].wait()
    omega = data_by_table(
        jnp.concatenate(
            [
                jnp.concatenate([s1r - s2r, -(s1i + s2i)], 1),
                jnp.concatenate([s1i - s2i, s1r + s2r], 1),
            ],
            0,
        ),
        (fermib[0], fermib[1]),
    )
    loads["wholeb"].wait()
    tb_g[...] = table_by_data((wholeb[0], wholeb[1]), omega).reshape(2, 16, 8, 512)
    for b in range(2):
        c_g[b] = exchange_o(planes_g(tb_g, b), rows_g(ub_g, b), some_g(ub_g, b))

    for b in range(2):
        c_v[b]()
        even, odd = ub_v[b, :128, :].T, ub_v[b, 128:, :].T
        for lo, value in ((0, even + odd), (1, even - odd)):
            for p in range(2):
                for h in range(4):
                    k = 64 * p + 16 * h
                    ta_v[b, 2 * h + lo, p] = value[k : k + 16]
        d_v[b] = exchange_z(ta_v.at[b], ua_v.at[b])
    for b in range(2):
        c_g[b]()
        for p in range(2):
            even, odd = ub_g[b, p, :128, :].T, ub_g[b, p, 128:, :].T
            for lo, value in ((0, even + odd), (1, even - odd)):
                for h in range(4):
                    ta_g[b, 2 * h + lo, p] = value[32 * h : 32 * h + 32]
        d_g[b] = exchange_z(ta_g.at[b], ua_g.at[b])

    loads["sheetb"].wait()
    for b in range(2):
        d_v[b]()
        sheet_back(ua_v.at[b], b, 16, sheetb, y_v)
    put_v = pltpu.make_async_copy(y_v, out_v, load_sem.at[30])
    put_v.start()
    for b in range(2):
        d_g[b]()
        sheet_back(ua_g.at[b], b, 32, sheetb, y_g)
    puts = [pltpu.make_async_copy(y_g.at[p, pl.ds(256 * h, 256)], out_g.at[p, pl.ds(256 * h, 256)], load_sem.at[31 + 2 * p + h]) for p in range(2) for h in range(2)]
    for put in puts:
        put.start()
    for copy in sent:
        copy.wait_send()
    put_v.wait()
    for put in puts:
        put.wait()


def hand_on(g, v, out_g, out_v, held_g, held_v, sem):
    ways = []
    for p in range(2):
        for half in range(2):
            ways.append([r.at[p, pl.ds(256 * half, 256)] for r in (g, held_g, out_g)])
        ways.append([r.at[p] for r in (v, held_v, out_v)])
    first = [pltpu.make_async_copy(a, b, sem.at[k]) for k, (a, b, _) in enumerate(ways)]
    second = [pltpu.make_async_copy(b, c, sem.at[6 + k]) for k, (_, b, c) in enumerate(ways)]
    for copy in first:
        copy.start()
    for there, back in zip(first, second):
        there.wait()
        back.start()
    for copy in second:
        copy.wait()


def view(x):
    n = x.shape[-3]
    return x.reshape(2, n, 2, 8, 128).transpose(0, 1, 3, 2, 4).reshape(2, n * 16, 128)


def unview(x):
    n = x.shape[1] // 16
    return x.reshape(2, n, 8, 2, 128).transpose(0, 1, 3, 2, 4).reshape(2, n, 2, 1024)


def per_device(green, inter):
    shapes = [
        (2, 512, 128), (2, 256, 128),
        (8, 2, 256, 256), (8, 2, 256, 256), (2, 256, 256), (2, 256, 256), (2, 256, 128), (2, 256, 128),
        (2, 512, 512), (2, 512, 512), (2, 512, 1024), (2, 1024, 512), (128, 128),
        (2, 8, 2, 32, 128), (2, 8, 2, 16, 128), (2, 8, 2, 32, 128), (2, 8, 2, 16, 128),
        (2, 2, 256, 128), (2, 256, 128), (2, 16, 8, 512), (16, 8, 512), (128, 1024),
        (2, 16, 8, 512), (16, 8, 512), (2, 2, 256, 128), (2, 256, 128),
        (2, 8, 2, 32, 128), (2, 8, 2, 16, 128), (2, 8, 2, 32, 128), (2, 8, 2, 16, 128), (2, 512, 128), (2, 256, 128),
    ]
    scratch = [pltpu.VMEM(s, BF16 if 2 <= k < 13 else F32) for k, s in enumerate(shapes)]
    any_spec = pl.BlockSpec(memory_space=pl.ANY)
    constants = tables()
    out_g, out_v = pl.pallas_call(
        kernel,
        out_shape=(
            jax.ShapeDtypeStruct((2, 512, 128), F32),
            jax.ShapeDtypeStruct((2, 256, 128), F32),
        ),
        in_specs=[any_spec] * (2 + len(constants)),
        out_specs=(any_spec, any_spec),
        scratch_shapes=scratch + [pltpu.SemaphoreType.DMA((36,)), pltpu.SemaphoreType.DMA((48,))],
        compiler_params=pltpu.CompilerParams(
            collective_id=0, has_side_effects=True, vmem_limit_bytes=56 << 20
        ),
    )(view(green), view(inter), *constants)
    out_g, out_v = pl.pallas_call(
        hand_on,
        out_shape=(jax.ShapeDtypeStruct((2, 512, 128), F32), jax.ShapeDtypeStruct((2, 256, 128), F32)),
        in_specs=[any_spec] * 2,
        out_specs=(any_spec, any_spec),
        scratch_shapes=[
            pltpu.VMEM((2, 512, 128), F32),
            pltpu.VMEM((2, 256, 128), F32),
            pltpu.SemaphoreType.DMA((12,)),
        ],
    )(out_g, out_v)
    return unview(out_g), unview(out_v)[None]


def solution(mesh):
    placed = (P(None, None, "freq", "kz", None), P(None, None, "freq", "kz", None))
    return jax.shard_map(
        per_device,
        mesh=mesh,
        in_specs=placed,
        out_specs=(P(None, "freq", "kz", None), P(None, None, "freq", "kz", None)),
        check_vma=False,
    )
```

```python
import functools
import math

import jax
import jax.numpy as jnp
import ml_dtypes
import numpy as np
from jax import lax
from jax.experimental import pallas as pl
from jax.experimental.pallas import tpu as pltpu
from jax.sharding import PartitionSpec as P

MESH = pl.DeviceIdType.MESH
F32 = jnp.float32
BF16 = jnp.bfloat16


def split_table(table):
    high = table.astype(ml_dtypes.bfloat16)
    low = (table - high.astype(np.float64)).astype(ml_dtypes.bfloat16)
    return np.stack([high, low])


def pairs_of(group):
    ys = range(32)

    def with_x(x):
        return [((x, y), ((32 - x) % 32, (32 - y) % 32)) for y in ys]

    if group == 0:
        pairs = []
        for x in (0, 16):
            pairs += [((x, 0), (x, 16))] + [((x, y), (x, 32 - y)) for y in range(1, 16)]
        return pairs + with_x(8)
    if group == 1:
        return with_x(4) + with_x(12)
    m = group // 2
    if group % 2 == 0:
        return with_x(m) + with_x(m + 8)
    return with_x(16 - m) + with_x(8 - m)


def columns(residue):
    if residue in (0, 4):
        return np.array(pairs_of(residue // 4))
    m = min(residue, 8 - residue)
    a, b = np.array(pairs_of(2 * m)), np.array(pairs_of(2 * m + 1))
    if residue < 4:
        return np.stack([a[:, 0], b[:, 1]], 1)
    return np.stack([b[:, 0], a[:, 1]], 1)


def sheet_tables():
    tables = []
    xl = np.repeat(np.arange(4), 32)
    ky = np.tile(np.arange(32), 4)
    for residue in range(8):
        site = columns(residue).reshape(2, 2, 16, 2, 2).transpose(0, 2, 1, 3, 4)
        x, y = site[..., 0], site[..., 1]
        assert (x % 8 == residue).all()
        turns = xl[:, None, None, None, None] * x + ky[:, None, None, None, None] * y
        angle = 2 * np.pi * (turns % 32) / 32
        c, s = np.cos(angle) / 32, np.sin(angle) / 32
        real = np.stack([c, s], 4)
        imag = np.stack([-s, c], 4)
        tables.append(np.concatenate([real, imag], 0).reshape(256, 256))
    return np.stack(tables)


def depth_tables():
    whole = np.zeros((2, 2, 16, 2, 16, 2, 2))
    kappa = np.arange(16)
    for parity in range(2):
        depth = 2 * np.arange(16) + parity
        angle = 2 * np.pi * ((depth[:, None] * kappa) % 32) / 32
        c, s = np.cos(angle) / math.sqrt(32), np.sin(angle) / math.sqrt(32)
        for e in range(2):
            whole[parity, 0, :, e, :, 0, e] = c
            whole[parity, 0, :, e, :, 1, e] = -s
            whole[parity, 1, :, e, :, 0, e] = s
            whole[parity, 1, :, e, :, 1, e] = c
    return whole.reshape(2, 64, 64)


def angles(length, offset):
    p = 2 * np.arange(length) - length + offset
    j = np.arange(256)
    return 2 * np.pi * ((p[:, None] * (2 * j + 1)) % 2048) / 2048


def fermi_table():
    theta = angles(512, 1).reshape(4, 4, 32, 256).transpose(1, 0, 2, 3).reshape(512, 256)
    return np.concatenate([np.cos(theta), np.sin(theta)], 1) / math.sqrt(512)


def bose_table():
    theta = angles(256, 0).reshape(4, 4, 16, 256).transpose(1, 0, 2, 3)
    table = np.zeros((2, 4, 2, 4, 16, 512))
    for parity in range(2):
        table[parity, :, parity] = np.concatenate([np.cos(theta), np.sin(theta)], -1)
    return table.reshape(2, 512, 512)


def mirror_tables():
    tables = np.zeros((2, 2, 32, 128))
    for parity in range(2):
        for same in range(2):
            for depth in range(16):
                other = (-depth - parity) % 16
                for e in range(2):
                    tables[parity, same, 2 * depth + e, 2 * other + (e if same else 1 - e)] = 1
    return tables.astype(ml_dtypes.bfloat16)


def by_parity(table):
    columns = max(128, table.shape[-1])
    wide = np.zeros(table.shape[:-1] + (columns,))
    wide[..., : table.shape[-1]] = table
    return np.ascontiguousarray(split_table(wide).swapaxes(0, 1))


@functools.cache
def tables():
    sheet = sheet_tables()
    whole = depth_tables()
    fermi = fermi_table()
    bose = bose_table()
    return (
        by_parity(sheet),
        by_parity(sheet.transpose(0, 2, 1)),
        by_parity(whole),
        by_parity(whole.transpose(0, 2, 1)),
        split_table(fermi),
        split_table(fermi.T),
        by_parity(bose / 16),
        by_parity(bose.transpose(0, 2, 1) / math.sqrt(512)),
        mirror_tables(),
    )


def split(x):
    high = x.astype(BF16)
    return high, (x - high.astype(F32)).astype(BF16)


def dot(a, b):
    return jnp.dot(a, b, preferred_element_type=F32)


def data_by_table(x, high_table, low_table):
    n = x.shape[0]
    high, low = split(x)
    both = dot(jnp.concatenate([high, low], 0), high_table)
    return both[:n] + both[n:] + dot(high, low_table)


def table_by_data(table, x):
    n, k = table.shape[1], x.shape[0]
    high, low = split(x)
    stacked = table[...].reshape(2 * n, 128)[:, :k]
    both = dot(stacked, high)
    return both[:n] + both[n:] + dot(stacked[:n], low)


def four(re, im, sign):
    s0r, s0i = re[0] + re[2], im[0] + im[2]
    d0r, d0i = re[0] - re[2], im[0] - im[2]
    s1r, s1i = re[1] + re[3], im[1] + im[3]
    d1r, d1i = re[1] - re[3], im[1] - im[3]
    tr, ti = (-d1i, d1r) if sign > 0 else (d1i, -d1r)
    return [s0r + s1r, d0r + tr, s0r - s1r, d0r - tr], [s0i + s1i, d0i + ti, s0i - s1i, d0i - ti]


def eight(re, im, sign):
    er, ei = four(re[0::2], im[0::2], sign)
    orr, oi = four(re[1::2], im[1::2], sign)
    h = math.sqrt(0.5)
    tr = [orr[0]]
    ti = [oi[0]]
    if sign > 0:
        tr += [h * (orr[1] - oi[1]), -oi[2], -h * (orr[3] + oi[3])]
        ti += [h * (orr[1] + oi[1]), orr[2], h * (orr[3] - oi[3])]
    else:
        tr += [h * (orr[1] + oi[1]), oi[2], h * (oi[3] - orr[3])]
        ti += [h * (oi[1] - orr[1]), -orr[2], -h * (orr[3] + oi[3])]
    return (
        [er[k] + tr[k] for k in range(4)] + [er[k] - tr[k] for k in range(4)],
        [ei[k] + ti[k] for k in range(4)] + [ei[k] - ti[k] for k in range(4)],
    )


FAR_FIRST = sorted(
    [(dx, dy, dc) for dx in range(4) for dy in range(4) for dc in range(2) if dx + dy + dc],
    key=lambda t: -(10 * min(t[0], 4 - t[0]) + 10 * min(t[1], 4 - t[1]) + t[2]),
)
ORDER = (0, 4, 1, 7, 2, 6, 3, 5)
PAIRS = ((1, 7, 2), (2, 6, 4), (3, 5, 6))


def lane(rows, columns):
    return lax.broadcasted_iota(jnp.int32, (rows, columns), 1)


def sheet_there(x_g, x_v, table, loads, out):
    def rows(p, g):
        return jnp.concatenate(
            [x[p, pl.ds(2 * g + b, n, 16), :] for b in range(2) for x, n in ((x_g, 32), (x_v, 16))], 0
        )

    yr, yi = eight([rows(0, g) for g in range(8)], [rows(1, g) for g in range(8)], 1)
    first = lane(96, 256) % 2 == 0
    plane = lane(48, 128) % 8 < 4

    def one(residue):
        loads["sheet" + str(residue)].wait()
        both = jnp.concatenate([yr[residue], yi[residue]], 1)
        return data_by_table(both, table[residue, 0], table[residue, 1])

    def put(group, value):
        for high in range(2):
            zero = value[:48, 128 * high : 128 * high + 128]
            one_ = value[48:, 128 * high : 128 * high + 128]
            out[2 * high, group] = jnp.where(plane, zero, pltpu.roll(one_, 4, 1))
            out[2 * high + 1, group] = jnp.where(plane, pltpu.roll(zero, 124, 1), one_)

    put(0, one(0))
    put(1, one(4))
    for m, n, group in PAIRS:
        a, b = one(m), one(n)
        put(group, jnp.where(first, a, b))
        put(group + 1, jnp.where(first, b, a))


def sheet_back(x, high, table):
    first = lane(96, 128) % 2 == 0
    plane = lane(48, 128) % 8 < 4

    def get(group):
        a, b = x[2 * high, group], x[2 * high + 1, group]
        return jnp.concatenate(
            [
                jnp.where(plane, a, pltpu.roll(b, 4, 1)),
                jnp.where(plane, pltpu.roll(a, 124, 1), b),
            ],
            0,
        )

    held = [None] * 8
    held[0], held[4] = get(0), get(1)
    for m, n, group in PAIRS:
        a, b = get(group), get(group + 1)
        held[m] = jnp.where(first, a, b)
        held[n] = jnp.where(first, b, a)
    part = pl.ds(128 * high, 128)
    return [data_by_table(held[k], table[k, 0, part, :], table[k, 1, part, :]) for k in range(8)]


def in_time(p, odd):
    ca, sa = p[:32, :256], p[:32, 256:]
    cb, sb = p[32:, :256], p[32:, 256:]
    if odd:
        return ca + sb, cb - sa, sb - ca, -(cb + sa)
    return ca + sb, cb - sa, ca - sb, cb + sa


def out_of_time(dr, di, er, ei):
    return jnp.concatenate([jnp.concatenate([dr, -ei], 1), jnp.concatenate([di, er], 1)], 0)


def kernel(
    green, inter, sheet_h, sheetb_h, whole_h, wholeb_h, fermi_h, fermib_h, bose_h, boseb_h, mirror_h,
    out_g, out_v,
    x_g, x_v, sheet, sheetb, whole, wholeb, fermi, fermib, bose, boseb, mirror,
    sa, ra, sb, rb, tb, ub, ta, ua, half, y_g, y_v, load_sem, put_sem, sem,
):
    kz, freq = lax.axis_index("kz"), lax.axis_index("freq")
    z_lo, c = kz // 8, kz % 8
    z_hi, y = freq // 4, freq % 4
    z = z_hi * 2 + z_lo
    o = c * 4 + y
    parity = o // 16

    loads = {}

    def load(name, src, dst):
        loads[name] = pltpu.make_async_copy(src, dst, load_sem.at[len(loads)])
        loads[name].start()

    for p in range(2):
        load("x_g" + str(p), green.at[p], x_g.at[p])
        load("x_v" + str(p), inter.at[p], x_v.at[p])
    for residue in ORDER:
        load("sheet" + str(residue), sheet_h.at[residue], sheet.at[residue])

    def z_peer(d):
        other = (z + d) % 8
        return other, {"kz": (other % 2) * 8 + c, "freq": (other // 2) * 4 + y}

    def near(dx, dy, dc):
        c2 = ((c // 2 + dx) % 4) * 2 + (c + dc) % 2
        y2 = (y + dy) % 4
        return c2 * 4 + y2, {"kz": z_lo * 8 + c2, "freq": z_hi * 4 + y2}

    barrier = pltpu.get_barrier_semaphore()
    for d in range(1, 8):
        pl.semaphore_signal(barrier, inc=1, device_id=z_peer(d)[1], device_id_type=MESH)
    for dx, dy, dc in FAR_FIRST:
        pl.semaphore_signal(barrier, inc=1, device_id=near(dx, dy, dc)[1], device_id_type=MESH)

    count = [0]

    def new_sem():
        count[0] += 1
        return sem.at[count[0] - 1]

    sent = []

    def exchange_z(src, dst):
        s, r, l = new_sem(), new_sem(), new_sem()
        own = pltpu.make_async_copy(src.at[z], dst.at[z], l)
        for d in (4, 3, 5, 2, 6, 1, 7):
            other, device = z_peer(d)
            pltpu.make_async_remote_copy(
                src.at[other], dst.at[z], s, r, device_id=device, device_id_type=MESH
            ).start()
        own.start()
        seven = pltpu.make_async_remote_copy(
            src.at[pl.ds(0, 7)], dst.at[pl.ds(0, 7)], s, r, device_id=z_peer(1)[1], device_id_type=MESH
        )
        sent.append(seven)

        def wait():
            seven.wait_recv()
            own.wait()

        return wait

    def exchange_o(src_at, dst_at, some):
        s, r, l = new_sem(), new_sem(), new_sem()
        own = pltpu.make_async_copy(src_at(o), dst_at(o), l)
        for dx, dy, dc in FAR_FIRST:
            other, device = near(dx, dy, dc)
            pltpu.make_async_remote_copy(
                src_at(other), dst_at(o), s, r, device_id=device, device_id_type=MESH
            ).start()
        own.start()
        rest = pltpu.make_async_remote_copy(
            some, some, s, r, device_id=near(0, 0, 1)[1], device_id_type=MESH
        )
        sent.append(rest)

        def wait():
            rest.wait_recv()
            own.wait()

        return wait

    def rows_at(ref, q):
        return lambda k: ref.at[q, k // 16, :, pl.ds(pl.multiple_of(k % 16 * 8, 8), 8), :]

    def planes_at(ref, q):
        return lambda k: ref.at[q, :, k // 4, :, pl.ds(pl.multiple_of(k % 4 * 128, 128), 128)]

    wait_a, wait_b, wait_c, wait_d = {}, {}, {}, {}

    def there(q):
        wait_a[q]()

        def of(lo, first, rows):
            return jnp.concatenate([ra[q, 2 * h + lo, first : first + rows] for h in range(4)], 0)

        even, odd = of(0, 0, 32), of(1, 0, 32)
        sb[q, 0, 0] = (even + odd).T
        sb[q, 1, 0] = (even - odd).T
        even, odd = of(0, 32, 16), of(1, 32, 16)
        turned = jnp.concatenate([even + odd, even - odd], 0).T
        sb[q, 0, 1] = turned
        sb[q, 1, 1] = turned
        wait_b[q] = exchange_o(rows_at(sb, q), planes_at(rb, q), other_way.at[q])

    def middle(q):
        wait_b[q]()
        if q == 0:
            for name in ("whole", "fermi0", "fermi1", "bose0", "bose1", "mirror"):
                loads[name].wait()
        both = jnp.concatenate([rb[q, 0].reshape(64, 512), rb[q, 1].reshape(64, 512)], 1)
        lattice = table_by_data(whole, both)
        g = in_time(data_by_table(lattice[:, :512], fermi[0], fermi[1]), True)
        v1r, v1i, v2r, v2i = in_time(data_by_table(lattice[:, 512:], bose[0], bose[1]), False)
        g1r, g1i, g2r, g2i = g
        same = jnp.where(jnp.logical_and(z == 0, o % 16 == 0), 1, 0) if q < 2 else 0
        turn = mirror[same][:, :32]
        high, low = split(jnp.concatenate(g, 1))
        turned = dot(turn, high) + dot(turn, low)
        m1r, m1i, m2r, m2i = [turned[:, 256 * k : 256 * k + 256] for k in range(4)]
        b1r, b1i = g1i * m2i - g1r * m2r, -(g1r * m2i + g1i * m2r)
        b2r, b2i = g2i * m1i - g2r * m1r, -(g2r * m1i + g2i * m1r)
        s1r, s1i = v1r * g1r - v1i * g1i, v1r * g1i + v1i * g1r
        s2r, s2i = v2r * g2r - v2i * g2i, v2r * g2i + v2i * g2r
        if q == 0:
            for name in ("fermib0", "fermib1", "boseb0", "boseb1", "wholeb"):
                loads[name].wait()
        omega = data_by_table(
            out_of_time(s1r - s2r, s1i - s2i, s1r + s2r, s1i + s2i), fermib[0], fermib[1]
        )
        nu = data_by_table(out_of_time(b1r + b2r, b1i + b2i, b1r - b2r, b1i - b2i), boseb[0], boseb[1])
        planes = table_by_data(wholeb, jnp.concatenate([omega, nu], 1))
        tb[q, 0] = planes[:, :512].reshape(8, 8, 512)
        tb[q, 1] = planes[:, 512:].reshape(8, 8, 512)
        wait_c[q] = exchange_o(planes_at(tb, q), rows_at(ub, q), other_way.at[q])

    def back(q):
        wait_c[q]()
        even, odd = ub[q, 0, 0].T, ub[q, 1, 0].T
        both = (ub[q, 0, 1] + ub[q, 1, 1]).T
        for lo in range(2):
            fermi_rows = even - odd if lo else even + odd
            bose_rows = both[:64] - both[64:] if lo else both[:64] + both[64:]
            for h in range(4):
                ta[q, 2 * h + lo, :32] = fermi_rows[32 * h : 32 * h + 32]
                ta[q, 2 * h + lo, 32:] = bose_rows[16 * h : 16 * h + 16]
        wait_d[q] = exchange_z(ta.at[q], ua.at[q])

    other_way = sb.reshape(4, 64, 8, 128).at[:, pl.ds(0, 62)]

    for name in ("x_g0", "x_g1", "x_v0", "x_v1"):
        loads[name].wait()
    sheet_there(x_g, x_v, sheet, loads, sa)
    pl.semaphore_wait(barrier, 38)
    for q in range(4):
        wait_a[q] = exchange_z(sa.at[q], ra.at[q])

    load("whole", whole_h.at[parity], whole)
    load("mirror", mirror_h.at[parity], mirror)
    for k in range(2):
        load("fermi" + str(k), fermi_h.at[k], fermi.at[k])
        load("bose" + str(k), bose_h.at[parity, k], bose.at[k])
    load("wholeb", wholeb_h.at[parity], wholeb)
    for k in range(2):
        load("fermib" + str(k), fermib_h.at[k], fermib.at[k])
        load("boseb" + str(k), boseb_h.at[parity, k], boseb.at[k])
    for k in range(2):
        load("sheetb" + str(k), sheetb_h.at[pl.ds(4 * k, 4)], sheetb.at[pl.ds(4 * k, 4)])

    there(0)
    there(1)
    middle(0)
    there(2)
    middle(1)
    back(0)
    there(3)
    middle(2)
    back(1)
    middle(3)
    back(2)
    back(3)

    loads["sheetb0"].wait()
    loads["sheetb1"].wait()
    wait_d[0]()
    wait_d[1]()
    for k, term in enumerate(sheet_back(ua, 0, sheetb)):
        half[k] = term
    wait_d[2]()
    wait_d[3]()
    terms = [half[k] + term for k, term in enumerate(sheet_back(ua, 1, sheetb))]
    re, im = eight([t[:, :128] for t in terms], [t[:, 128:] for t in terms], -1)
    for p, part in enumerate((re, im)):
        for g in range(8):
            for b in range(2):
                y_g[p, pl.ds(2 * g + b, 32, 16), :] = part[g][48 * b : 48 * b + 32]
                y_v[p, pl.ds(2 * g + b, 16, 16), :] = part[g][48 * b + 32 : 48 * b + 48]
    puts = []
    for p in range(2):
        for h in range(2):
            rows = pl.ds(256 * h, 256)
            puts.append(pltpu.make_async_copy(y_g.at[p, rows], out_g.at[p, rows], put_sem.at[len(puts)]))
        puts.append(pltpu.make_async_copy(y_v.at[p], out_v.at[p], put_sem.at[len(puts)]))
    for put in puts:
        put.start()
    for copy in sent:
        copy.wait_send()
    for put in puts:
        put.wait()


def hand_on(g, v, out_g, out_v, held_g, held_v, sem):
    ways = []
    for p in range(2):
        for half in range(2):
            ways.append([r.at[p, pl.ds(256 * half, 256)] for r in (g, held_g, out_g)])
        ways.append([r.at[p] for r in (v, held_v, out_v)])
    first = [pltpu.make_async_copy(a, b, sem.at[k]) for k, (a, b, _) in enumerate(ways)]
    second = [pltpu.make_async_copy(b, c, sem.at[6 + k]) for k, (_, b, c) in enumerate(ways)]
    for copy in first:
        copy.start()
    for there, back in zip(first, second):
        there.wait()
        back.start()
    for copy in second:
        copy.wait()


def view(x):
    n = x.shape[-3]
    return x.reshape(2, n, 2, 8, 128).transpose(0, 1, 3, 2, 4).reshape(2, n * 16, 128)


def unview(x):
    n = x.shape[1] // 16
    return x.reshape(2, n, 8, 2, 128).transpose(0, 1, 3, 2, 4).reshape(2, n, 2, 1024)


def per_device(green, inter):
    shapes = [
        (2, 512, 128), (2, 256, 128),
        (8, 2, 256, 256), (8, 2, 256, 256), (2, 64, 128), (2, 64, 128),
        (2, 512, 512), (2, 512, 512), (2, 512, 512), (2, 512, 512), (2, 32, 128),
        (4, 8, 48, 128), (4, 8, 48, 128), (4, 2, 2, 128, 128), (4, 2, 8, 8, 512),
        (4, 2, 8, 8, 512), (4, 2, 2, 128, 128), (4, 8, 48, 128), (4, 8, 48, 128),
        (8, 96, 256), (2, 512, 128), (2, 256, 128),
    ]
    scratch = [pltpu.VMEM(s, BF16 if 2 <= k < 11 else F32) for k, s in enumerate(shapes)]
    any_spec = pl.BlockSpec(memory_space=pl.ANY)
    constants = tables()
    out_g, out_v = pl.pallas_call(
        kernel,
        out_shape=(
            jax.ShapeDtypeStruct((2, 512, 128), F32),
            jax.ShapeDtypeStruct((2, 256, 128), F32),
        ),
        in_specs=[any_spec] * (2 + len(constants)),
        out_specs=(any_spec, any_spec),
        scratch_shapes=scratch + [pltpu.SemaphoreType.DMA((n,)) for n in (26, 6, 48)],
        compiler_params=pltpu.CompilerParams(
            collective_id=0, has_side_effects=True, vmem_limit_bytes=56 << 20
        ),
    )(view(green), view(inter), *constants)
    out_g, out_v = pl.pallas_call(
        hand_on,
        out_shape=(jax.ShapeDtypeStruct((2, 512, 128), F32), jax.ShapeDtypeStruct((2, 256, 128), F32)),
        in_specs=[any_spec] * 2,
        out_specs=(any_spec, any_spec),
        scratch_shapes=[
            pltpu.VMEM((2, 512, 128), F32),
            pltpu.VMEM((2, 256, 128), F32),
            pltpu.SemaphoreType.DMA((12,)),
        ],
    )(out_g, out_v)
    return unview(out_g), unview(out_v)[None]


def solution(mesh):
    placed = (P(None, None, "freq", "kz", None), P(None, None, "freq", "kz", None))
    return jax.shard_map(
        per_device,
        mesh=mesh,
        in_specs=placed,
        out_specs=(P(None, "freq", "kz", None), P(None, None, "freq", "kz", None)),
        check_vma=False,
    )
```

```python
import functools
import math

import jax
import jax.numpy as jnp
import ml_dtypes
import numpy as np
from jax import lax
from jax.experimental import pallas as pl
from jax.experimental.pallas import tpu as pltpu
from jax.sharding import PartitionSpec as P

MESH = pl.DeviceIdType.MESH
F32 = jnp.float32
BF16 = jnp.bfloat16


def split_table(table):
    high = table.astype(ml_dtypes.bfloat16)
    low = (table - high.astype(np.float64)).astype(ml_dtypes.bfloat16)
    return np.stack([high, low])


def pairs_of(group):
    ys = range(32)

    def with_x(x):
        return [((x, y), ((32 - x) % 32, (32 - y) % 32)) for y in ys]

    if group == 0:
        pairs = []
        for x in (0, 16):
            pairs += [((x, 0), (x, 16))] + [((x, y), (x, 32 - y)) for y in range(1, 16)]
        return pairs + with_x(8)
    if group == 1:
        return with_x(4) + with_x(12)
    m = group // 2
    if group % 2 == 0:
        return with_x(m) + with_x(m + 8)
    return with_x(16 - m) + with_x(8 - m)


def columns(residue):
    if residue in (0, 4):
        return np.array(pairs_of(residue // 4))
    m = min(residue, 8 - residue)
    a, b = np.array(pairs_of(2 * m)), np.array(pairs_of(2 * m + 1))
    if residue < 4:
        return np.stack([a[:, 0], b[:, 1]], 1)
    return np.stack([b[:, 0], a[:, 1]], 1)


def sheet_tables():
    tables = []
    xl = np.repeat(np.arange(4), 32)
    ky = np.tile(np.arange(32), 4)
    for residue in range(8):
        site = columns(residue).reshape(2, 2, 16, 2, 2).transpose(0, 2, 1, 3, 4)
        x, y = site[..., 0], site[..., 1]
        assert (x % 8 == residue).all()
        turns = xl[:, None, None, None, None] * x + ky[:, None, None, None, None] * y
        angle = 2 * np.pi * (turns % 32) / 32
        c, s = np.cos(angle) / 32, np.sin(angle) / 32
        real = np.stack([c, s], 4)
        imag = np.stack([-s, c], 4)
        tables.append(np.concatenate([real, imag], 0).reshape(256, 256))
    return np.stack(tables)


def depth_tables():
    whole = np.zeros((2, 2, 16, 2, 16, 2, 2))
    kappa = np.arange(16)
    for parity in range(2):
        depth = 2 * np.arange(16) + parity
        angle = 2 * np.pi * ((depth[:, None] * kappa) % 32) / 32
        c, s = np.cos(angle) / math.sqrt(32), np.sin(angle) / math.sqrt(32)
        for e in range(2):
            whole[parity, 0, :, e, :, 0, e] = c
            whole[parity, 0, :, e, :, 1, e] = -s
            whole[parity, 1, :, e, :, 0, e] = s
            whole[parity, 1, :, e, :, 1, e] = c
    return whole.reshape(2, 64, 64)


def angles(length, offset):
    p = 2 * np.arange(length) - length + offset
    j = np.arange(256)
    return 2 * np.pi * ((p[:, None] * (2 * j + 1)) % 2048) / 2048


def fermi_table():
    theta = angles(512, 1).reshape(4, 4, 32, 256).transpose(1, 0, 2, 3).reshape(512, 256)
    return np.concatenate([np.cos(theta), np.sin(theta)], 1) / math.sqrt(512)


def bose_table():
    theta = angles(256, 0).reshape(4, 4, 16, 256).transpose(1, 0, 2, 3)
    table = np.zeros((2, 4, 2, 4, 16, 512))
    for parity in range(2):
        table[parity, :, parity] = np.concatenate([np.cos(theta), np.sin(theta)], -1)
    return table.reshape(2, 512, 512)


def mirror_tables():
    tables = np.zeros((2, 2, 32, 128))
    for parity in range(2):
        for same in range(2):
            for depth in range(16):
                other = (-depth - parity) % 16
                for e in range(2):
                    tables[parity, same, 2 * depth + e, 2 * other + (e if same else 1 - e)] = 1
    return tables.astype(ml_dtypes.bfloat16)


def by_parity(table):
    columns = max(128, table.shape[-1])
    wide = np.zeros(table.shape[:-1] + (columns,))
    wide[..., : table.shape[-1]] = table
    return np.ascontiguousarray(split_table(wide).swapaxes(0, 1))


@functools.cache
def tables():
    sheet = sheet_tables()
    whole = depth_tables()
    fermi = fermi_table()
    bose = bose_table()
    return (
        by_parity(sheet),
        by_parity(sheet.transpose(0, 2, 1)),
        by_parity(whole),
        by_parity(whole.transpose(0, 2, 1)),
        split_table(fermi),
        split_table(fermi.T),
        by_parity(bose / 16),
        by_parity(bose.transpose(0, 2, 1) / math.sqrt(512)),
        mirror_tables(),
    )


def split(x):
    high = x.astype(BF16)
    return high, (x - high.astype(F32)).astype(BF16)


def dot(a, b):
    return jnp.dot(a, b, preferred_element_type=F32)


def data_by_table(x, high_table, low_table):
    n = x.shape[0]
    high, low = split(x)
    both = dot(jnp.concatenate([high, low], 0), high_table)
    return both[:n] + both[n:] + dot(high, low_table)


def table_by_data(table, x):
    n, k = table.shape[1], x.shape[0]
    high, low = split(x)
    stacked = table[...].reshape(2 * n, 128)[:, :k]
    both = dot(stacked, high)
    return both[:n] + both[n:] + dot(stacked[:n], low)


def four(re, im, sign):
    s0r, s0i = re[0] + re[2], im[0] + im[2]
    d0r, d0i = re[0] - re[2], im[0] - im[2]
    s1r, s1i = re[1] + re[3], im[1] + im[3]
    d1r, d1i = re[1] - re[3], im[1] - im[3]
    tr, ti = (-d1i, d1r) if sign > 0 else (d1i, -d1r)
    return [s0r + s1r, d0r + tr, s0r - s1r, d0r - tr], [s0i + s1i, d0i + ti, s0i - s1i, d0i - ti]


def eight(re, im, sign):
    er, ei = four(re[0::2], im[0::2], sign)
    orr, oi = four(re[1::2], im[1::2], sign)
    h = math.sqrt(0.5)
    tr = [orr[0]]
    ti = [oi[0]]
    if sign > 0:
        tr += [h * (orr[1] - oi[1]), -oi[2], -h * (orr[3] + oi[3])]
        ti += [h * (orr[1] + oi[1]), orr[2], h * (orr[3] - oi[3])]
    else:
        tr += [h * (orr[1] + oi[1]), oi[2], h * (oi[3] - orr[3])]
        ti += [h * (oi[1] - orr[1]), -orr[2], -h * (orr[3] + oi[3])]
    return (
        [er[k] + tr[k] for k in range(4)] + [er[k] - tr[k] for k in range(4)],
        [ei[k] + ti[k] for k in range(4)] + [ei[k] - ti[k] for k in range(4)],
    )


FAR_FIRST = sorted(
    [(dx, dy, dc) for dx in range(4) for dy in range(4) for dc in range(2) if dx + dy + dc],
    key=lambda t: -(10 * min(t[0], 4 - t[0]) + 10 * min(t[1], 4 - t[1]) + t[2]),
)
ORDER = (0, 4, 1, 7, 2, 6, 3, 5)
PAIRS = ((1, 7, 2), (2, 6, 4), (3, 5, 6))


def lane(rows, columns):
    return lax.broadcasted_iota(jnp.int32, (rows, columns), 1)


def sheet_there(x_g, x_v, table, loads, out):
    def rows(p, g):
        return jnp.concatenate(
            [x[p, pl.ds(2 * g + b, n, 16), :] for b in range(2) for x, n in ((x_g, 32), (x_v, 16))], 0
        )

    yr, yi = eight([rows(0, g) for g in range(8)], [rows(1, g) for g in range(8)], 1)
    first = lane(96, 256) % 2 == 0
    plane = lane(48, 128) % 8 < 4

    def one(residue):
        loads["sheet" + str(residue)].wait()
        both = jnp.concatenate([yr[residue], yi[residue]], 1)
        return data_by_table(both, table[residue, 0], table[residue, 1])

    def put(group, value):
        for high in range(2):
            zero = value[:48, 128 * high : 128 * high + 128]
            one_ = value[48:, 128 * high : 128 * high + 128]
            out[2 * high, group] = jnp.where(plane, zero, pltpu.roll(one_, 4, 1))
            out[2 * high + 1, group] = jnp.where(plane, pltpu.roll(zero, 124, 1), one_)

    put(0, one(0))
    put(1, one(4))
    for m, n, group in PAIRS:
        a, b = one(m), one(n)
        put(group, jnp.where(first, a, b))
        put(group + 1, jnp.where(first, b, a))


def sheet_back(x, high, table):
    first = lane(96, 128) % 2 == 0
    plane = lane(48, 128) % 8 < 4

    def get(group):
        a, b = x[2 * high, group], x[2 * high + 1, group]
        return jnp.concatenate(
            [
                jnp.where(plane, a, pltpu.roll(b, 4, 1)),
                jnp.where(plane, pltpu.roll(a, 124, 1), b),
            ],
            0,
        )

    held = [None] * 8
    held[0], held[4] = get(0), get(1)
    for m, n, group in PAIRS:
        a, b = get(group), get(group + 1)
        held[m] = jnp.where(first, a, b)
        held[n] = jnp.where(first, b, a)
    part = pl.ds(128 * high, 128)
    return [data_by_table(held[k], table[k, 0, part, :], table[k, 1, part, :]) for k in range(8)]


def in_time(p, odd):
    ca, sa = p[:32, :256], p[:32, 256:]
    cb, sb = p[32:, :256], p[32:, 256:]
    if odd:
        return ca + sb, cb - sa, sb - ca, -(cb + sa)
    return ca + sb, cb - sa, ca - sb, cb + sa


def out_of_time(dr, di, er, ei):
    return jnp.concatenate([jnp.concatenate([dr, -ei], 1), jnp.concatenate([di, er], 1)], 0)


def kernel(
    green, inter, sheet_h, sheetb_h, whole_h, wholeb_h, fermi_h, fermib_h, bose_h, boseb_h, mirror_h,
    out_g, out_v,
    x_g, x_v, sheet, sheetb, whole, wholeb, fermi, fermib, bose, boseb, mirror,
    sa, ra, sb, rb, tb, ub, ta, ua, half, load_sem, sem,
):
    kz, freq = lax.axis_index("kz"), lax.axis_index("freq")
    z_lo, c = kz // 8, kz % 8
    z_hi, y = freq // 4, freq % 4
    z = z_hi * 2 + z_lo
    o = c * 4 + y
    parity = o // 16

    loads = {}

    def load(name, src, dst):
        loads[name] = pltpu.make_async_copy(src, dst, load_sem.at[len(loads)])
        loads[name].start()

    for p in range(2):
        load("x_g" + str(p), green.at[p], x_g.at[p])
        load("x_v" + str(p), inter.at[p], x_v.at[p])
    for residue in ORDER:
        load("sheet" + str(residue), sheet_h.at[residue], sheet.at[residue])

    def z_peer(d):
        other = (z + d) % 8
        return other, {"kz": (other % 2) * 8 + c, "freq": (other // 2) * 4 + y}

    def near(dx, dy, dc):
        c2 = ((c // 2 + dx) % 4) * 2 + (c + dc) % 2
        y2 = (y + dy) % 4
        return c2 * 4 + y2, {"kz": z_lo * 8 + c2, "freq": z_hi * 4 + y2}

    barrier = pltpu.get_barrier_semaphore()
    for d in range(1, 8):
        pl.semaphore_signal(barrier, inc=1, device_id=z_peer(d)[1], device_id_type=MESH)
    for dx, dy, dc in FAR_FIRST:
        pl.semaphore_signal(barrier, inc=1, device_id=near(dx, dy, dc)[1], device_id_type=MESH)

    count = [0]

    def new_sem():
        count[0] += 1
        return sem.at[count[0] - 1]

    sent = []

    def exchange_z(src, dst):
        s, r, l = new_sem(), new_sem(), new_sem()
        own = pltpu.make_async_copy(src.at[z], dst.at[z], l)
        for d in (4, 3, 5, 2, 6, 1, 7):
            other, device = z_peer(d)
            pltpu.make_async_remote_copy(
                src.at[other], dst.at[z], s, r, device_id=device, device_id_type=MESH
            ).start()
        own.start()
        seven = pltpu.make_async_remote_copy(
            src.at[pl.ds(0, 7)], dst.at[pl.ds(0, 7)], s, r, device_id=z_peer(1)[1], device_id_type=MESH
        )
        sent.append(seven)

        def wait():
            seven.wait_recv()
            own.wait()

        return wait

    def exchange_o(src_at, dst_at, some):
        s, r, l = new_sem(), new_sem(), new_sem()
        own = pltpu.make_async_copy(src_at(o), dst_at(o), l)
        for dx, dy, dc in FAR_FIRST:
            other, device = near(dx, dy, dc)
            pltpu.make_async_remote_copy(
                src_at(other), dst_at(o), s, r, device_id=device, device_id_type=MESH
            ).start()
        own.start()
        rest = pltpu.make_async_remote_copy(
            some, some, s, r, device_id=near(0, 0, 1)[1], device_id_type=MESH
        )
        sent.append(rest)

        def wait():
            rest.wait_recv()
            own.wait()

        return wait

    def rows_at(ref, q):
        return lambda k: ref.at[q, k // 16, :, pl.ds(pl.multiple_of(k % 16 * 8, 8), 8), :]

    def planes_at(ref, q):
        return lambda k: ref.at[q, :, k // 4, :, pl.ds(pl.multiple_of(k % 4 * 128, 128), 128)]

    wait_a, wait_b, wait_c, wait_d = {}, {}, {}, {}

    def there(q):
        wait_a[q]()

        def of(lo, first, rows):
            return jnp.concatenate([ra[q, 2 * h + lo, first : first + rows] for h in range(4)], 0)

        even, odd = of(0, 0, 32), of(1, 0, 32)
        sb[q, 0, 0] = (even + odd).T
        sb[q, 1, 0] = (even - odd).T
        even, odd = of(0, 32, 16), of(1, 32, 16)
        turned = jnp.concatenate([even + odd, even - odd], 0).T
        sb[q, 0, 1] = turned
        sb[q, 1, 1] = turned
        wait_b[q] = exchange_o(rows_at(sb, q), planes_at(rb, q), other_way.at[q])

    def middle(q):
        wait_b[q]()
        if q == 0:
            for name in ("whole", "fermi0", "fermi1", "bose0", "bose1", "mirror"):
                loads[name].wait()
        both = jnp.concatenate([rb[q, 0].reshape(64, 512), rb[q, 1].reshape(64, 512)], 1)
        lattice = table_by_data(whole, both)
        g = in_time(data_by_table(lattice[:, :512], fermi[0], fermi[1]), True)
        v1r, v1i, v2r, v2i = in_time(data_by_table(lattice[:, 512:], bose[0], bose[1]), False)
        g1r, g1i, g2r, g2i = g
        same = jnp.where(jnp.logical_and(z == 0, o % 16 == 0), 1, 0) if q < 2 else 0
        turn = mirror[same][:, :32]
        high, low = split(jnp.concatenate(g, 1))
        turned = dot(turn, high) + dot(turn, low)
        m1r, m1i, m2r, m2i = [turned[:, 256 * k : 256 * k + 256] for k in range(4)]
        b1r, b1i = g1i * m2i - g1r * m2r, -(g1r * m2i + g1i * m2r)
        b2r, b2i = g2i * m1i - g2r * m1r, -(g2r * m1i + g2i * m1r)
        s1r, s1i = v1r * g1r - v1i * g1i, v1r * g1i + v1i * g1r
        s2r, s2i = v2r * g2r - v2i * g2i, v2r * g2i + v2i * g2r
        if q == 0:
            for name in ("fermib0", "fermib1", "boseb0", "boseb1", "wholeb"):
                loads[name].wait()
        omega = data_by_table(
            out_of_time(s1r - s2r, s1i - s2i, s1r + s2r, s1i + s2i), fermib[0], fermib[1]
        )
        nu = data_by_table(out_of_time(b1r + b2r, b1i + b2i, b1r - b2r, b1i - b2i), boseb[0], boseb[1])
        planes = table_by_data(wholeb, jnp.concatenate([omega, nu], 1))
        tb[q, 0] = planes[:, :512].reshape(8, 8, 512)
        tb[q, 1] = planes[:, 512:].reshape(8, 8, 512)
        wait_c[q] = exchange_o(planes_at(tb, q), rows_at(ub, q), other_way.at[q])

    def back(q):
        wait_c[q]()
        even, odd = ub[q, 0, 0].T, ub[q, 1, 0].T
        both = (ub[q, 0, 1] + ub[q, 1, 1]).T
        for lo in range(2):
            fermi_rows = even - odd if lo else even + odd
            bose_rows = both[:64] - both[64:] if lo else both[:64] + both[64:]
            for h in range(4):
                ta[q, 2 * h + lo, :32] = fermi_rows[32 * h : 32 * h + 32]
                ta[q, 2 * h + lo, 32:] = bose_rows[16 * h : 16 * h + 16]
        wait_d[q] = exchange_z(ta.at[q], ua.at[q])

    other_way = sb.reshape(4, 64, 8, 128).at[:, pl.ds(0, 62)]

    for name in ("x_g0", "x_g1", "x_v0", "x_v1"):
        loads[name].wait()
    sheet_there(x_g, x_v, sheet, loads, sa)
    pl.semaphore_wait(barrier, 38)
    for q in range(4):
        wait_a[q] = exchange_z(sa.at[q], ra.at[q])

    load("whole", whole_h.at[parity], whole)
    load("mirror", mirror_h.at[parity], mirror)
    for k in range(2):
        load("fermi" + str(k), fermi_h.at[k], fermi.at[k])
        load("bose" + str(k), bose_h.at[parity, k], bose.at[k])
    load("wholeb", wholeb_h.at[parity], wholeb)
    for k in range(2):
        load("fermib" + str(k), fermib_h.at[k], fermib.at[k])
        load("boseb" + str(k), boseb_h.at[parity, k], boseb.at[k])
    for k in range(2):
        load("sheetb" + str(k), sheetb_h.at[pl.ds(4 * k, 4)], sheetb.at[pl.ds(4 * k, 4)])

    there(0)
    there(1)
    middle(0)
    there(2)
    middle(1)
    back(0)
    there(3)
    middle(2)
    back(1)
    middle(3)
    back(2)
    back(3)

    loads["sheetb0"].wait()
    loads["sheetb1"].wait()
    wait_d[0]()
    wait_d[1]()
    for k, term in enumerate(sheet_back(ua, 0, sheetb)):
        half[k] = term
    wait_d[2]()
    wait_d[3]()
    terms = [half[k] + term for k, term in enumerate(sheet_back(ua, 1, sheetb))]
    re, im = eight([t[:, :128] for t in terms], [t[:, 128:] for t in terms], -1)
    for p, part in enumerate((re, im)):
        for g in range(8):
            for b in range(2):
                out_g[p, pl.ds(2 * g + b, 32, 16), :] = part[g][48 * b : 48 * b + 32]
                out_v[p, pl.ds(2 * g + b, 16, 16), :] = part[g][48 * b + 32 : 48 * b + 48]
    for copy in sent:
        copy.wait_send()


def hand_on(g, v, out_g, out_v, sem):
    ways = []
    for p in range(2):
        for half in range(2):
            ways.append([r.at[p, pl.ds(256 * half, 256)] for r in (g, out_g)])
        ways.append([r.at[p] for r in (v, out_v)])
    copies = [pltpu.make_async_copy(a, b, sem.at[k]) for k, (a, b) in enumerate(ways)]
    for copy in copies:
        copy.start()
    for copy in copies:
        copy.wait()


def view(x):
    n = x.shape[-3]
    return x.reshape(2, n, 2, 8, 128).transpose(0, 1, 3, 2, 4).reshape(2, n * 16, 128)


def unview(x):
    n = x.shape[1] // 16
    return x.reshape(2, n, 8, 2, 128).transpose(0, 1, 3, 2, 4).reshape(2, n, 2, 1024)


def per_device(green, inter):
    shapes = [
        (2, 512, 128), (2, 256, 128),
        (8, 2, 256, 256), (8, 2, 256, 256), (2, 64, 128), (2, 64, 128),
        (2, 512, 512), (2, 512, 512), (2, 512, 512), (2, 512, 512), (2, 32, 128),
        (4, 8, 48, 128), (4, 8, 48, 128), (4, 2, 2, 128, 128), (4, 2, 8, 8, 512),
        (4, 2, 8, 8, 512), (4, 2, 2, 128, 128), (4, 8, 48, 128), (4, 8, 48, 128),
        (8, 96, 256),
    ]
    scratch = [pltpu.VMEM(s, BF16 if 2 <= k < 11 else F32) for k, s in enumerate(shapes)]
    any_spec = pl.BlockSpec(memory_space=pl.ANY)
    vmem_spec = pl.BlockSpec(memory_space=pltpu.VMEM)
    constants = tables()
    out_g, out_v = pl.pallas_call(
        kernel,
        out_shape=(pltpu.VMEM((2, 512, 128), F32), pltpu.VMEM((2, 256, 128), F32)),
        in_specs=[any_spec] * (2 + len(constants)),
        out_specs=(vmem_spec, vmem_spec),
        scratch_shapes=scratch + [pltpu.SemaphoreType.DMA((n,)) for n in (26, 48)],
        compiler_params=pltpu.CompilerParams(
            collective_id=0, has_side_effects=True, vmem_limit_bytes=56 << 20
        ),
    )(view(green), view(inter), *constants)
    out_g, out_v = pl.pallas_call(
        hand_on,
        out_shape=(jax.ShapeDtypeStruct((2, 512, 128), F32), jax.ShapeDtypeStruct((2, 256, 128), F32)),
        in_specs=[vmem_spec] * 2,
        out_specs=(any_spec, any_spec),
        scratch_shapes=[pltpu.SemaphoreType.DMA((6,))],
    )(*[pltpu.with_memory_space_constraint(x, pltpu.VMEM) for x in (out_g, out_v)])
    return unview(out_g), unview(out_v)[None]


def solution(mesh):
    placed = (P(None, None, "freq", "kz", None), P(None, None, "freq", "kz", None))
    return jax.shard_map(
        per_device,
        mesh=mesh,
        in_specs=placed,
        out_specs=(P(None, "freq", "kz", None), P(None, None, "freq", "kz", None)),
        check_vma=False,
    )
```

```python
import functools
import math

import jax
import jax.numpy as jnp
import ml_dtypes
import numpy as np
from jax import lax
from jax.experimental import pallas as pl
from jax.experimental.pallas import tpu as pltpu
from jax.sharding import PartitionSpec as P

MESH = pl.DeviceIdType.MESH
F32 = jnp.float32
BF16 = jnp.bfloat16


def split_table(table):
    high = table.astype(ml_dtypes.bfloat16)
    low = (table - high.astype(np.float64)).astype(ml_dtypes.bfloat16)
    return np.stack([high, low])


def pairs_of(group):
    ys = range(32)

    def with_x(x):
        return [((x, y), ((32 - x) % 32, (32 - y) % 32)) for y in ys]

    if group == 0:
        pairs = []
        for x in (0, 16):
            pairs += [((x, 0), (x, 16))] + [((x, y), (x, 32 - y)) for y in range(1, 16)]
        return pairs + with_x(8)
    if group == 1:
        return with_x(4) + with_x(12)
    m = group // 2
    if group % 2 == 0:
        return with_x(m) + with_x(m + 8)
    return with_x(16 - m) + with_x(8 - m)


def columns(residue):
    if residue in (0, 4):
        return np.array(pairs_of(residue // 4))
    m = min(residue, 8 - residue)
    a, b = np.array(pairs_of(2 * m)), np.array(pairs_of(2 * m + 1))
    if residue < 4:
        return np.stack([a[:, 0], b[:, 1]], 1)
    return np.stack([b[:, 0], a[:, 1]], 1)


def sheet_tables():
    tables = []
    xl = np.repeat(np.arange(4), 32)
    ky = np.tile(np.arange(32), 4)
    for residue in range(8):
        site = columns(residue).reshape(2, 2, 16, 2, 2).transpose(0, 1, 3, 2, 4)
        x, y = site[..., 0], site[..., 1]
        assert (x % 8 == residue).all()
        turns = xl[:, None, None, None, None] * x + ky[:, None, None, None, None] * y
        angle = 2 * np.pi * (turns % 32) / 32
        c, s = np.cos(angle) / 32, np.sin(angle) / 32
        real = np.stack([c, s], 3)
        imag = np.stack([-s, c], 3)
        tables.append(np.concatenate([real, imag], 0).reshape(256, 256))
    return np.stack(tables)


def depth_tables():
    whole = np.zeros((2, 96, 96))
    kappa = np.arange(16)
    depth = np.arange(16)
    for parity in range(2):
        angle = 2 * np.pi * (((2 * depth[:, None] + parity) * kappa) % 32) / 32
        c, s = np.cos(angle) / math.sqrt(32), np.sin(angle) / math.sqrt(32)
        parts = [[c, -s], [s, c]]
        for new in range(2):
            for old in range(2):
                for b in range(2):
                    block = parts[new][old][:, b::2]
                    for e in range(2):
                        row = new * 32 + e * 16
                        whole[parity, row : row + 16, b * 4 + old * 2 + e :: 12] = block
                    row = 64 + new * 16
                    whole[parity, row : row + 16, 8 + b * 2 + old :: 12] = block
    return whole


def angles(length, offset):
    p = 2 * np.arange(length) - length + offset
    j = np.arange(256)
    return 2 * np.pi * ((p[:, None] * (2 * j + 1)) % 2048) / 2048


def fermi_table():
    theta = angles(512, 1).reshape(4, 4, 32, 256).transpose(1, 0, 2, 3).reshape(512, 256)
    return np.concatenate([np.cos(theta), np.sin(theta)], 1) / math.sqrt(512)


def bose_table():
    theta = angles(256, 0).reshape(4, 4, 16, 256).transpose(1, 0, 2, 3).reshape(256, 256)
    return np.concatenate([np.cos(theta), np.sin(theta)], 1)


def mirror_tables():
    tables = np.zeros((2, 2, 32, 128))
    for parity in range(2):
        for same in range(2):
            for depth in range(16):
                other = (-depth - parity) % 16
                for e in range(2):
                    f = e if same else 1 - e
                    tables[parity, same, 16 * e + depth, 16 * f + other] = 1
    return tables.astype(ml_dtypes.bfloat16)


def by_parity(table):
    columns = max(128, table.shape[-1])
    wide = np.zeros(table.shape[:-1] + (columns,))
    wide[..., : table.shape[-1]] = table
    return np.ascontiguousarray(split_table(wide).swapaxes(0, 1))


@functools.cache
def tables():
    sheet = sheet_tables()
    whole = depth_tables()
    fermi = fermi_table()
    bose = bose_table()
    return (
        by_parity(sheet),
        by_parity(sheet.transpose(0, 2, 1)),
        by_parity(whole),
        by_parity(whole.transpose(0, 2, 1)),
        split_table(fermi),
        split_table(fermi.T),
        split_table(bose / 16),
        split_table(bose.T / math.sqrt(512)),
        mirror_tables(),
    )


def split(x):
    high = x.astype(BF16)
    return high, (x - high.astype(F32)).astype(BF16)


def dot(a, b):
    return jnp.dot(a, b, preferred_element_type=F32)


def data_by_table(x, high_table, low_table):
    n = x.shape[0]
    high, low = split(x)
    both = dot(jnp.concatenate([high, low], 0), high_table)
    return both[:n] + both[n:] + dot(high, low_table)


def table_by_data(table, x):
    n, k = table.shape[1], x.shape[0]
    high, low = split(x)
    stacked = table[...].reshape(2 * n, 128)[:, :k]
    both = dot(stacked, high)
    return both[:n] + both[n:] + dot(stacked[:n], low)


def four(re, im, sign):
    s0r, s0i = re[0] + re[2], im[0] + im[2]
    d0r, d0i = re[0] - re[2], im[0] - im[2]
    s1r, s1i = re[1] + re[3], im[1] + im[3]
    d1r, d1i = re[1] - re[3], im[1] - im[3]
    tr, ti = (-d1i, d1r) if sign > 0 else (d1i, -d1r)
    return [s0r + s1r, d0r + tr, s0r - s1r, d0r - tr], [s0i + s1i, d0i + ti, s0i - s1i, d0i - ti]


def eight(re, im, sign):
    er, ei = four(re[0::2], im[0::2], sign)
    orr, oi = four(re[1::2], im[1::2], sign)
    h = math.sqrt(0.5)
    tr = [orr[0]]
    ti = [oi[0]]
    if sign > 0:
        tr += [h * (orr[1] - oi[1]), -oi[2], -h * (orr[3] + oi[3])]
        ti += [h * (orr[1] + oi[1]), orr[2], h * (orr[3] - oi[3])]
    else:
        tr += [h * (orr[1] + oi[1]), oi[2], h * (oi[3] - orr[3])]
        ti += [h * (oi[1] - orr[1]), -orr[2], -h * (orr[3] + oi[3])]
    return (
        [er[k] + tr[k] for k in range(4)] + [er[k] - tr[k] for k in range(4)],
        [ei[k] + ti[k] for k in range(4)] + [ei[k] - ti[k] for k in range(4)],
    )


FAR_FIRST = sorted(
    [(dx, dy, dc) for dx in range(4) for dy in range(4) for dc in range(2) if dx + dy + dc],
    key=lambda t: -(10 * min(t[0], 4 - t[0]) + 10 * min(t[1], 4 - t[1]) + t[2]),
)
ORDER = (0, 4, 1, 7, 2, 6, 3, 5)
PAIRS = ((1, 7, 2), (2, 6, 4), (3, 5, 6))


def lane(rows, columns):
    return lax.broadcasted_iota(jnp.int32, (rows, columns), 1)


def sheet_there(x_g, x_v, table, loads, out):
    def rows(p, g):
        return jnp.concatenate(
            [x[p, pl.ds(2 * g + b, n, 16), :] for b in range(2) for x, n in ((x_g, 32), (x_v, 16))], 0
        )

    yr, yi = eight([rows(0, g) for g in range(8)], [rows(1, g) for g in range(8)], 1)
    first = lane(96, 256) // 16 % 2 == 0
    plane = lane(48, 128) < 64

    def one(residue):
        loads["sheet" + str(residue)].wait()
        both = jnp.concatenate([yr[residue], yi[residue]], 1)
        return data_by_table(both, table[residue, 0], table[residue, 1])

    def put(group, value):
        for high in range(2):
            zero = value[:48, 128 * high : 128 * high + 128]
            one_ = value[48:, 128 * high : 128 * high + 128]
            out[2 * high, group] = jnp.where(plane, zero, pltpu.roll(one_, 64, 1))
            out[2 * high + 1, group] = jnp.where(plane, pltpu.roll(zero, 64, 1), one_)

    put(0, one(0))
    put(1, one(4))
    for m, n, group in PAIRS:
        a, b = one(m), one(n)
        put(group, jnp.where(first, a, b))
        put(group + 1, jnp.where(first, b, a))


def sheet_back(x, high, table):
    first = lane(96, 128) // 16 % 2 == 0
    plane = lane(48, 128) < 64

    def get(group):
        a, b = x[2 * high, group], x[2 * high + 1, group]
        return jnp.concatenate(
            [
                jnp.where(plane, a, pltpu.roll(b, 64, 1)),
                jnp.where(plane, pltpu.roll(a, 64, 1), b),
            ],
            0,
        )

    held = [None] * 8
    held[0], held[4] = get(0), get(1)
    for m, n, group in PAIRS:
        a, b = get(group), get(group + 1)
        held[m] = jnp.where(first, a, b)
        held[n] = jnp.where(first, b, a)
    part = pl.ds(128 * high, 128)
    return [data_by_table(held[k], table[k, 0, part, :], table[k, 1, part, :]) for k in range(8)]


def apart(x):
    rows, columns = x.shape
    lower = lane(rows, 128) < 64
    ones, twos = [], []
    for k in range(0, columns, 256):
        a, b = x[:, k : k + 128], x[:, k + 128 : k + 256]
        ones.append(jnp.where(lower, a, pltpu.roll(b, 64, 1)))
        twos.append(jnp.where(lower, pltpu.roll(a, 64, 1), b))
    return jnp.concatenate(ones, 1), jnp.concatenate(twos, 1)


def together(ones, twos):
    lower = lane(ones.shape[0], 128) < 64
    pieces = []
    for k in range(0, ones.shape[1], 128):
        a, b = ones[:, k : k + 128], twos[:, k : k + 128]
        pieces.append(jnp.where(lower, a, pltpu.roll(b, 64, 1)))
        pieces.append(jnp.where(lower, pltpu.roll(a, 64, 1), b))
    return jnp.concatenate(pieces, 1)


def in_time(p, odd):
    ca, sa = p[:32, :256], p[:32, 256:]
    cb, sb = p[32:, :256], p[32:, 256:]
    if odd:
        return ca + sb, cb - sa, sb - ca, -(cb + sa)
    return ca + sb, cb - sa, ca - sb, cb + sa


def out_of_time(dr, di, er, ei):
    return jnp.concatenate([jnp.concatenate([dr, -ei], 1), jnp.concatenate([di, er], 1)], 0)


def kernel(
    green, inter, sheet_h, sheetb_h, whole_h, wholeb_h, fermi_h, fermib_h, bose_h, boseb_h, mirror_h,
    out_g, out_v,
    x_g, x_v, sheet, sheetb, whole, wholeb, fermi, fermib, bose, boseb, mirror,
    sa, ra, sb, rb, tb, ub, ta, ua, half, load_sem, sem,
):
    kz, freq = lax.axis_index("kz"), lax.axis_index("freq")
    z_lo, c = kz // 8, kz % 8
    z_hi, y = freq // 4, freq % 4
    z = z_hi * 2 + z_lo
    o = c * 4 + y
    parity = o // 16

    loads = {}

    def load(name, src, dst):
        loads[name] = pltpu.make_async_copy(src, dst, load_sem.at[len(loads)])
        loads[name].start()

    for p in range(2):
        load("x_g" + str(p), green.at[p], x_g.at[p])
        load("x_v" + str(p), inter.at[p], x_v.at[p])
    for residue in ORDER:
        load("sheet" + str(residue), sheet_h.at[residue], sheet.at[residue])

    def z_peer(d):
        other = (z + d) % 8
        return other, {"kz": (other % 2) * 8 + c, "freq": (other // 2) * 4 + y}

    def near(dx, dy, dc):
        c2 = ((c // 2 + dx) % 4) * 2 + (c + dc) % 2
        y2 = (y + dy) % 4
        return c2 * 4 + y2, {"kz": z_lo * 8 + c2, "freq": z_hi * 4 + y2}

    barrier = pltpu.get_barrier_semaphore()
    for d in range(1, 8):
        pl.semaphore_signal(barrier, inc=1, device_id=z_peer(d)[1], device_id_type=MESH)
    for dx, dy, dc in FAR_FIRST:
        pl.semaphore_signal(barrier, inc=1, device_id=near(dx, dy, dc)[1], device_id_type=MESH)

    count = [0]

    def new_sem():
        count[0] += 1
        return sem.at[count[0] - 1]

    sent = []

    def exchange_z(src, dst):
        s, r, l = new_sem(), new_sem(), new_sem()
        own = pltpu.make_async_copy(src.at[z], dst.at[z], l)
        for d in (4, 3, 5, 2, 6, 1, 7):
            other, device = z_peer(d)
            pltpu.make_async_remote_copy(
                src.at[other], dst.at[z], s, r, device_id=device, device_id_type=MESH
            ).start()
        own.start()
        seven = pltpu.make_async_remote_copy(
            src.at[pl.ds(0, 7)], dst.at[pl.ds(0, 7)], s, r, device_id=z_peer(1)[1], device_id_type=MESH
        )
        sent.append(seven)

        def wait():
            seven.wait_recv()
            own.wait()

        return wait

    def exchange_o(src_at, dst_at, some):
        s, r, l = new_sem(), new_sem(), new_sem()
        own = pltpu.make_async_copy(src_at(o), dst_at(o), l)
        for dx, dy, dc in FAR_FIRST:
            other, device = near(dx, dy, dc)
            pltpu.make_async_remote_copy(
                src_at(other), dst_at(o), s, r, device_id=device, device_id_type=MESH
            ).start()
        own.start()
        rest = pltpu.make_async_remote_copy(
            some, some, s, r, device_id=near(0, 0, 1)[1], device_id_type=MESH
        )
        sent.append(rest)

        def wait():
            rest.wait_recv()
            own.wait()

        return wait

    def rows_at(ref, q):
        return lambda k: ref.at[q, k // 16, pl.ds(pl.multiple_of(k % 16 * 12, 4), 12), :]

    def planes_at(ref, q):
        return lambda k: ref.at[q, k % 4, pl.ds(pl.multiple_of(k // 4 * 12, 4), 12), :]

    wait_a, wait_b, wait_c, wait_d = {}, {}, {}, {}

    def there(q):
        wait_a[q]()

        def of(lo, first, rows):
            return jnp.concatenate([ra[q, 2 * h + lo, first : first + rows] for h in range(4)], 0)

        even, odd = of(0, 0, 32), of(1, 0, 32)
        for k, value in enumerate(((even + odd).T, (even - odd).T)):
            for r in range(8):
                sb[q, k, pl.ds(r, 16, 12), :] = value[16 * r : 16 * r + 16]
        even, odd = of(0, 32, 16), of(1, 32, 16)
        value = jnp.concatenate([even + odd, even - odd], 0).T
        for r in range(4):
            one, two = value[32 * r : 32 * r + 16], value[32 * r + 16 : 32 * r + 32]
            sb[q, 0, pl.ds(8 + r, 16, 12), :] = jnp.where(lower, one, pltpu.roll(two, 64, 1))
            sb[q, 1, pl.ds(8 + r, 16, 12), :] = jnp.where(lower, pltpu.roll(one, 64, 1), two)
        wait_b[q] = exchange_o(rows_at(sb, q), planes_at(rb, q), other_way)

    def middle(q):
        wait_b[q]()
        if q == 0:
            for name in ("whole", "fermi0", "fermi1", "bose0", "bose1", "mirror"):
                loads[name].wait()
        lattice = table_by_data(whole, jnp.concatenate([rb[q, k] for k in range(4)], 1))
        g = in_time(data_by_table(lattice[:64], fermi[0], fermi[1]), True)
        one, two = apart(lattice[64:])
        v = jnp.concatenate([one[:16], two[:16], one[16:], two[16:]], 0)
        v1r, v1i, v2r, v2i = in_time(data_by_table(v, bose[0], bose[1]), False)
        g1r, g1i, g2r, g2i = g
        same = jnp.where(jnp.logical_and(z == 0, o % 16 == 0), 1, 0) if q < 2 else 0
        turn = mirror[same][:, :32]
        high, low = split(jnp.concatenate(g, 1))
        turned = dot(turn, high) + dot(turn, low)
        m1r, m1i, m2r, m2i = [turned[:, 256 * k : 256 * k + 256] for k in range(4)]
        b1r, b1i = g1i * m2i - g1r * m2r, -(g1r * m2i + g1i * m2r)
        b2r, b2i = g2i * m1i - g2r * m1r, -(g2r * m1i + g2i * m1r)
        s1r, s1i = v1r * g1r - v1i * g1i, v1r * g1i + v1i * g1r
        s2r, s2i = v2r * g2r - v2i * g2i, v2r * g2i + v2i * g2r
        if q == 0:
            for name in ("fermib0", "fermib1", "boseb0", "boseb1", "wholeb"):
                loads[name].wait()
        omega = data_by_table(
            out_of_time(s1r - s2r, s1i - s2i, s1r + s2r, s1i + s2i), fermib[0], fermib[1]
        )
        nu = data_by_table(out_of_time(b1r + b2r, b1i + b2i, b1r - b2r, b1i - b2i), boseb[0], boseb[1])
        nu = together(
            jnp.concatenate([nu[:16], nu[32:48]], 0), jnp.concatenate([nu[16:32], nu[48:]], 0)
        )
        planes = table_by_data(wholeb, jnp.concatenate([omega, nu], 0))
        for k in range(4):
            tb[q, k] = planes[:, 128 * k : 128 * k + 128]
        wait_c[q] = exchange_o(planes_at(tb, q), rows_at(ub, q), other_way)

    def back(q):
        wait_c[q]()
        even, odd = [
            jnp.concatenate([ub[q, k, pl.ds(r, 16, 12), :] for r in range(8)], 0).T for k in range(2)
        ]
        pieces = []
        for r in range(4):
            one, two = [ub[q, k, pl.ds(8 + r, 16, 12), :] for k in range(2)]
            pieces.append(jnp.where(lower, one, pltpu.roll(two, 64, 1)))
            pieces.append(jnp.where(lower, pltpu.roll(one, 64, 1), two))
        both = jnp.concatenate(pieces, 0).T
        for lo in range(2):
            fermi_rows = even - odd if lo else even + odd
            bose_rows = both[:64] - both[64:] if lo else both[:64] + both[64:]
            for h in range(4):
                ta[q, 2 * h + lo, :32] = fermi_rows[32 * h : 32 * h + 32]
                ta[q, 2 * h + lo, 32:] = bose_rows[16 * h : 16 * h + 16]
        wait_d[q] = exchange_z(ta.at[q], ua.at[q])

    other_way = x_g.at[0, pl.ds(0, 372)]
    lower = lane(16, 128) < 64

    for name in ("x_g0", "x_g1", "x_v0", "x_v1"):
        loads[name].wait()
    sheet_there(x_g, x_v, sheet, loads, sa)
    pl.semaphore_wait(barrier, 38)
    for q in range(4):
        wait_a[q] = exchange_z(sa.at[q], ra.at[q])

    load("whole", whole_h.at[parity], whole)
    load("mirror", mirror_h.at[parity], mirror)
    for k in range(2):
        load("fermi" + str(k), fermi_h.at[k], fermi.at[k])
        load("bose" + str(k), bose_h.at[k], bose.at[k])
    load("wholeb", wholeb_h.at[parity], wholeb)
    for k in range(2):
        load("fermib" + str(k), fermib_h.at[k], fermib.at[k])
        load("boseb" + str(k), boseb_h.at[k], boseb.at[k])
    for k in range(2):
        load("sheetb" + str(k), sheetb_h.at[pl.ds(4 * k, 4)], sheetb.at[pl.ds(4 * k, 4)])

    there(0)
    there(1)
    middle(0)
    there(2)
    middle(1)
    back(0)
    there(3)
    middle(2)
    back(1)
    middle(3)
    back(2)
    back(3)

    loads["sheetb0"].wait()
    loads["sheetb1"].wait()
    wait_d[0]()
    wait_d[1]()
    for k, term in enumerate(sheet_back(ua, 0, sheetb)):
        half[k] = term
    wait_d[2]()
    wait_d[3]()
    terms = [half[k] + term for k, term in enumerate(sheet_back(ua, 1, sheetb))]
    re, im = eight([t[:, :128] for t in terms], [t[:, 128:] for t in terms], -1)
    for p, part in enumerate((re, im)):
        for g in range(8):
            for b in range(2):
                out_g[p, pl.ds(2 * g + b, 32, 16), :] = part[g][48 * b : 48 * b + 32]
                out_v[p, pl.ds(2 * g + b, 16, 16), :] = part[g][48 * b + 32 : 48 * b + 48]
    for copy in sent:
        copy.wait_send()


def hand_on(g, v, out_g, out_v, sem):
    ways = []
    for p in range(2):
        for half in range(2):
            ways.append([r.at[p, pl.ds(256 * half, 256)] for r in (g, out_g)])
        ways.append([r.at[p] for r in (v, out_v)])
    copies = [pltpu.make_async_copy(a, b, sem.at[k]) for k, (a, b) in enumerate(ways)]
    for copy in copies:
        copy.start()
    for copy in copies:
        copy.wait()


def view(x):
    n = x.shape[-3]
    return x.reshape(2, n, 2, 8, 128).transpose(0, 1, 3, 2, 4).reshape(2, n * 16, 128)


def unview(x):
    n = x.shape[1] // 16
    return x.reshape(2, n, 8, 2, 128).transpose(0, 1, 3, 2, 4).reshape(2, n, 2, 1024)


def per_device(green, inter):
    shapes = [
        (2, 512, 128), (2, 256, 128),
        (8, 2, 256, 256), (8, 2, 256, 256), (2, 96, 128), (2, 96, 128),
        (2, 512, 512), (2, 512, 512), (2, 256, 512), (2, 512, 256), (2, 32, 128),
        (4, 8, 48, 128), (4, 8, 48, 128), (4, 2, 192, 128), (4, 4, 96, 128),
        (4, 4, 96, 128), (4, 2, 192, 128), (4, 8, 48, 128), (4, 8, 48, 128),
        (8, 96, 256),
    ]
    scratch = [pltpu.VMEM(s, BF16 if 2 <= k < 11 else F32) for k, s in enumerate(shapes)]
    any_spec = pl.BlockSpec(memory_space=pl.ANY)
    vmem_spec = pl.BlockSpec(memory_space=pltpu.VMEM)
    constants = tables()
    out_g, out_v = pl.pallas_call(
        kernel,
        out_shape=(pltpu.VMEM((2, 512, 128), F32), pltpu.VMEM((2, 256, 128), F32)),
        in_specs=[any_spec] * (2 + len(constants)),
        out_specs=(vmem_spec, vmem_spec),
        scratch_shapes=scratch + [pltpu.SemaphoreType.DMA((n,)) for n in (26, 48)],
        compiler_params=pltpu.CompilerParams(
            collective_id=0, has_side_effects=True, vmem_limit_bytes=56 << 20
        ),
    )(view(green), view(inter), *constants)
    out_g, out_v = pl.pallas_call(
        hand_on,
        out_shape=(jax.ShapeDtypeStruct((2, 512, 128), F32), jax.ShapeDtypeStruct((2, 256, 128), F32)),
        in_specs=[vmem_spec] * 2,
        out_specs=(any_spec, any_spec),
        scratch_shapes=[pltpu.SemaphoreType.DMA((6,))],
    )(*[pltpu.with_memory_space_constraint(x, pltpu.VMEM) for x in (out_g, out_v)])
    return unview(out_g), unview(out_v)[None]


def solution(mesh):
    placed = (P(None, None, "freq", "kz", None), P(None, None, "freq", "kz", None))
    return jax.shard_map(
        per_device,
        mesh=mesh,
        in_specs=placed,
        out_specs=(P(None, "freq", "kz", None), P(None, None, "freq", "kz", None)),
        check_vma=False,
    )
```

```python
import functools
import math

import jax
import jax.numpy as jnp
import ml_dtypes
import numpy as np
from jax import lax
from jax.experimental import pallas as pl
from jax.experimental.pallas import tpu as pltpu
from jax.sharding import PartitionSpec as P

MESH = pl.DeviceIdType.MESH
F32 = jnp.float32
BF16 = jnp.bfloat16


def split_table(table):
    high = table.astype(ml_dtypes.bfloat16)
    low = (table - high.astype(np.float64)).astype(ml_dtypes.bfloat16)
    return np.stack([high, low])


def pairs_of(group):
    ys = range(32)

    def with_x(x):
        return [((x, y), ((32 - x) % 32, (32 - y) % 32)) for y in ys]

    if group == 0:
        pairs = []
        for x in (0, 16):
            pairs += [((x, 0), (x, 16))] + [((x, y), (x, 32 - y)) for y in range(1, 16)]
        return pairs + with_x(8)
    if group == 1:
        return with_x(4) + with_x(12)
    m = group // 2
    if group % 2 == 0:
        return with_x(m) + with_x(m + 8)
    return with_x(16 - m) + with_x(8 - m)


def columns(residue):
    if residue in (0, 4):
        return np.array(pairs_of(residue // 4))
    m = min(residue, 8 - residue)
    a, b = np.array(pairs_of(2 * m)), np.array(pairs_of(2 * m + 1))
    if residue < 4:
        return np.stack([a[:, 0], b[:, 1]], 1)
    return np.stack([b[:, 0], a[:, 1]], 1)


def sheet_tables():
    tables = []
    xl = np.repeat(np.arange(4), 32)
    ky = np.tile(np.arange(32), 4)
    for residue in range(8):
        site = columns(residue).reshape(2, 2, 16, 2, 2).transpose(0, 1, 3, 2, 4)
        x, y = site[..., 0], site[..., 1]
        assert (x % 8 == residue).all()
        turns = xl[:, None, None, None, None] * x + ky[:, None, None, None, None] * y
        angle = 2 * np.pi * (turns % 32) / 32
        c, s = np.cos(angle) / 32, np.sin(angle) / 32
        real = np.stack([c, s], 3)
        imag = np.stack([-s, c], 3)
        tables.append(np.concatenate([real, imag], 0).reshape(256, 256))
    return np.stack(tables)


def depth_tables():
    whole = np.zeros((2, 96, 96))
    kappa = np.arange(16)
    depth = np.arange(16)
    for parity in range(2):
        angle = 2 * np.pi * (((2 * depth[:, None] + parity) * kappa) % 32) / 32
        c, s = np.cos(angle) / math.sqrt(32), np.sin(angle) / math.sqrt(32)
        parts = [[c, -s], [s, c]]
        for new in range(2):
            for old in range(2):
                for b in range(2):
                    block = parts[new][old][:, b::2]
                    for e in range(2):
                        row = new * 32 + e * 16
                        whole[parity, row : row + 16, b * 4 + old * 2 + e :: 12] = block
                    row = 64 + new * 16
                    whole[parity, row : row + 16, 8 + b * 2 + old :: 12] = block
    return whole


def angles(length, offset):
    p = 2 * np.arange(length) - length + offset
    j = np.arange(256)
    return 2 * np.pi * ((p[:, None] * (2 * j + 1)) % 2048) / 2048


def fermi_table():
    theta = angles(512, 1).reshape(4, 4, 32, 256).transpose(1, 0, 2, 3).reshape(512, 256)
    return np.concatenate([np.cos(theta), np.sin(theta)], 1) / math.sqrt(512)


def bose_table():
    theta = angles(256, 0).reshape(4, 4, 16, 256).transpose(1, 0, 2, 3).reshape(256, 256)
    return np.concatenate([np.cos(theta), np.sin(theta)], 1)


def mirror_tables():
    tables = np.zeros((2, 2, 32, 128))
    for parity in range(2):
        for same in range(2):
            for depth in range(16):
                other = (-depth - parity) % 16
                for e in range(2):
                    f = e if same else 1 - e
                    tables[parity, same, 16 * e + depth, 16 * f + other] = 1
    return tables.astype(ml_dtypes.bfloat16)


def by_parity(table):
    columns = max(128, table.shape[-1])
    wide = np.zeros(table.shape[:-1] + (columns,))
    wide[..., : table.shape[-1]] = table
    return np.ascontiguousarray(split_table(wide).swapaxes(0, 1))


@functools.cache
def tables():
    sheet = sheet_tables()
    whole = depth_tables()
    fermi = fermi_table()
    bose = bose_table()
    return (
        by_parity(sheet),
        by_parity(sheet.transpose(0, 2, 1)),
        by_parity(whole),
        by_parity(whole.transpose(0, 2, 1)),
        split_table(fermi),
        split_table(fermi.T),
        split_table(bose / 16),
        split_table(bose.T / math.sqrt(512)),
        mirror_tables(),
    )


def split(x):
    high = x.astype(BF16)
    return high, (x - high.astype(F32)).astype(BF16)


def dot(a, b):
    return jnp.dot(a, b, preferred_element_type=F32)


def data_by_table(x, high_table, low_table):
    n = x.shape[0]
    high, low = split(x)
    both = dot(jnp.concatenate([high, low], 0), high_table)
    return both[:n] + both[n:] + dot(high, low_table)


def table_by_data(table, x):
    n, k = table.shape[1], x.shape[0]
    high, low = split(x)
    stacked = table[...].reshape(2 * n, 128)[:, :k]
    both = dot(stacked, high)
    return both[:n] + both[n:] + dot(stacked[:n], low)


def four(re, im, sign):
    s0r, s0i = re[0] + re[2], im[0] + im[2]
    d0r, d0i = re[0] - re[2], im[0] - im[2]
    s1r, s1i = re[1] + re[3], im[1] + im[3]
    d1r, d1i = re[1] - re[3], im[1] - im[3]
    tr, ti = (-d1i, d1r) if sign > 0 else (d1i, -d1r)
    return [s0r + s1r, d0r + tr, s0r - s1r, d0r - tr], [s0i + s1i, d0i + ti, s0i - s1i, d0i - ti]


def eight(re, im, sign):
    er, ei = four(re[0::2], im[0::2], sign)
    orr, oi = four(re[1::2], im[1::2], sign)
    h = math.sqrt(0.5)
    tr = [orr[0]]
    ti = [oi[0]]
    if sign > 0:
        tr += [h * (orr[1] - oi[1]), -oi[2], -h * (orr[3] + oi[3])]
        ti += [h * (orr[1] + oi[1]), orr[2], h * (orr[3] - oi[3])]
    else:
        tr += [h * (orr[1] + oi[1]), oi[2], h * (oi[3] - orr[3])]
        ti += [h * (oi[1] - orr[1]), -orr[2], -h * (orr[3] + oi[3])]
    return (
        [er[k] + tr[k] for k in range(4)] + [er[k] - tr[k] for k in range(4)],
        [ei[k] + ti[k] for k in range(4)] + [ei[k] - ti[k] for k in range(4)],
    )


FAR_FIRST = sorted(
    [(dx, dy, dc) for dx in range(4) for dy in range(4) for dc in range(2) if dx + dy + dc],
    key=lambda t: -(10 * min(t[0], 4 - t[0]) + 10 * min(t[1], 4 - t[1]) + t[2]),
)
ORDER = (0, 4, 1, 7, 2, 6, 3, 5)
PAIRS = ((1, 7, 2), (2, 6, 4), (3, 5, 6))


def lane(rows, columns):
    return lax.broadcasted_iota(jnp.int32, (rows, columns), 1)


def sheet_there(x_g, x_v, table, loads, out):
    def rows(p, g):
        return jnp.concatenate(
            [x[p, pl.ds(2 * g + b, n, 16), :] for b in range(2) for x, n in ((x_g, 32), (x_v, 16))], 0
        )

    yr, yi = eight([rows(0, g) for g in range(8)], [rows(1, g) for g in range(8)], 1)
    first = lane(96, 256) // 16 % 2 == 0
    plane = lane(48, 128) < 64

    def one(residue):
        loads["sheet" + str(residue)].wait()
        both = jnp.concatenate([yr[residue], yi[residue]], 1)
        return data_by_table(both, table[residue, 0], table[residue, 1])

    def put(group, value):
        for high in range(2):
            zero = value[:48, 128 * high : 128 * high + 128]
            one_ = value[48:, 128 * high : 128 * high + 128]
            out[2 * high, group] = jnp.where(plane, zero, pltpu.roll(one_, 64, 1))
            out[2 * high + 1, group] = jnp.where(plane, pltpu.roll(zero, 64, 1), one_)

    put(0, one(0))
    put(1, one(4))
    for m, n, group in PAIRS:
        a, b = one(m), one(n)
        put(group, jnp.where(first, a, b))
        put(group + 1, jnp.where(first, b, a))


def sheet_back(x, high, table):
    first = lane(96, 128) // 16 % 2 == 0
    plane = lane(48, 128) < 64

    def get(group):
        a, b = x[2 * high, group], x[2 * high + 1, group]
        return jnp.concatenate(
            [
                jnp.where(plane, a, pltpu.roll(b, 64, 1)),
                jnp.where(plane, pltpu.roll(a, 64, 1), b),
            ],
            0,
        )

    held = [None] * 8
    held[0], held[4] = get(0), get(1)
    for m, n, group in PAIRS:
        a, b = get(group), get(group + 1)
        held[m] = jnp.where(first, a, b)
        held[n] = jnp.where(first, b, a)
    part = pl.ds(128 * high, 128)
    return [data_by_table(held[k], table[k, 0, part, :], table[k, 1, part, :]) for k in range(8)]


def apart(x):
    rows, columns = x.shape
    lower = lane(rows, 128) < 64
    ones, twos = [], []
    for k in range(0, columns, 256):
        a, b = x[:, k : k + 128], x[:, k + 128 : k + 256]
        ones.append(jnp.where(lower, a, pltpu.roll(b, 64, 1)))
        twos.append(jnp.where(lower, pltpu.roll(a, 64, 1), b))
    return jnp.concatenate(ones, 1), jnp.concatenate(twos, 1)


def together(ones, twos):
    lower = lane(ones.shape[0], 128) < 64
    pieces = []
    for k in range(0, ones.shape[1], 128):
        a, b = ones[:, k : k + 128], twos[:, k : k + 128]
        pieces.append(jnp.where(lower, a, pltpu.roll(b, 64, 1)))
        pieces.append(jnp.where(lower, pltpu.roll(a, 64, 1), b))
    return jnp.concatenate(pieces, 1)


def in_time(p, odd):
    ca, sa = p[:32, :256], p[:32, 256:]
    cb, sb = p[32:, :256], p[32:, 256:]
    if odd:
        return ca + sb, cb - sa, sb - ca, -(cb + sa)
    return ca + sb, cb - sa, ca - sb, cb + sa


def out_of_time(dr, di, er, ei):
    return jnp.concatenate([jnp.concatenate([dr, -ei], 1), jnp.concatenate([di, er], 1)], 0)


def kernel(
    green, inter, sheet_h, sheetb_h, whole_h, wholeb_h, fermi_h, fermib_h, bose_h, boseb_h, mirror_h,
    out_g, out_v,
    x_g, x_v, sheet, sheetb, whole, wholeb, fermi, fermib, bose, boseb, mirror,
    sa, ra, sb, rb, tb, ub, ta, ua, half, load_sem, sem,
):
    kz, freq = lax.axis_index("kz"), lax.axis_index("freq")
    z_lo, c = kz // 8, kz % 8
    z_hi, y = freq // 4, freq % 4
    z = z_hi * 2 + z_lo
    o = c * 4 + y
    parity = o // 16

    loads = {}

    def load(name, src, dst):
        loads[name] = pltpu.make_async_copy(src, dst, load_sem.at[len(loads)])
        loads[name].start()

    for p in range(2):
        load("x_g" + str(p), green.at[p], x_g.at[p])
        load("x_v" + str(p), inter.at[p], x_v.at[p])
    for residue in ORDER:
        load("sheet" + str(residue), sheet_h.at[residue], sheet.at[residue])

    def z_peer(d):
        other = (z + d) % 8
        return other, {"kz": (other % 2) * 8 + c, "freq": (other // 2) * 4 + y}

    def near(dx, dy, dc):
        c2 = ((c // 2 + dx) % 4) * 2 + (c + dc) % 2
        y2 = (y + dy) % 4
        return c2 * 4 + y2, {"kz": z_lo * 8 + c2, "freq": z_hi * 4 + y2}

    barrier = pltpu.get_barrier_semaphore()
    for d in range(1, 8):
        pl.semaphore_signal(barrier, inc=1, device_id=z_peer(d)[1], device_id_type=MESH)
    for dx, dy, dc in FAR_FIRST:
        pl.semaphore_signal(barrier, inc=1, device_id=near(dx, dy, dc)[1], device_id_type=MESH)

    count = [0]

    def new_sem():
        count[0] += 1
        return sem.at[count[0] - 1]

    sent = []

    def exchange_z(src, dst):
        s, r, l = new_sem(), new_sem(), new_sem()
        own = pltpu.make_async_copy(src.at[z], dst.at[z], l)
        for d in (4, 3, 5, 2, 6, 1, 7):
            other, device = z_peer(d)
            pltpu.make_async_remote_copy(
                src.at[other], dst.at[z], s, r, device_id=device, device_id_type=MESH
            ).start()
        own.start()
        seven = pltpu.make_async_remote_copy(
            src.at[pl.ds(0, 7)], dst.at[pl.ds(0, 7)], s, r, device_id=z_peer(1)[1], device_id_type=MESH
        )
        sent.append(seven)

        def wait():
            seven.wait_recv()
            own.wait()

        return wait

    def exchange_o(src_at, dst_at, some):
        s, r, l = new_sem(), new_sem(), new_sem()
        own = pltpu.make_async_copy(src_at(o), dst_at(o), l)
        for dx, dy, dc in FAR_FIRST:
            other, device = near(dx, dy, dc)
            pltpu.make_async_remote_copy(
                src_at(other), dst_at(o), s, r, device_id=device, device_id_type=MESH
            ).start()
        own.start()
        rest = pltpu.make_async_remote_copy(
            some, some, s, r, device_id=near(0, 0, 1)[1], device_id_type=MESH
        )
        sent.append(rest)

        def wait():
            rest.wait_recv()
            own.wait()

        return wait

    def rows_at(ref, q):
        return lambda k: ref.at[q, k // 16, pl.ds(pl.multiple_of(k % 16 * 12, 4), 12), :]

    def planes_at(ref, q):
        return lambda k: ref.at[q, k % 4, pl.ds(pl.multiple_of(k // 4 * 12, 4), 12), :]

    wait_a, wait_b, wait_c, wait_d = {}, {}, {}, {}

    def there(q):
        wait_a[q]()

        def of(lo, first, rows):
            return jnp.concatenate([ra[q, 2 * h + lo, first : first + rows] for h in range(4)], 0)

        even, odd = of(0, 0, 32), of(1, 0, 32)
        for k, value in enumerate(((even + odd).T, (even - odd).T)):
            for r in range(8):
                sb[q, k, pl.ds(r, 16, 12), :] = value[16 * r : 16 * r + 16]
        even, odd = of(0, 32, 16), of(1, 32, 16)
        value = jnp.concatenate([even + odd, even - odd], 0).T
        for r in range(4):
            one, two = value[32 * r : 32 * r + 16], value[32 * r + 16 : 32 * r + 32]
            sb[q, 0, pl.ds(8 + r, 16, 12), :] = jnp.where(lower, one, pltpu.roll(two, 64, 1))
            sb[q, 1, pl.ds(8 + r, 16, 12), :] = jnp.where(lower, pltpu.roll(one, 64, 1), two)
        wait_b[q] = exchange_o(rows_at(sb, q), planes_at(rb, q), other_way)

    def middle(q):
        wait_b[q]()
        if q == 0:
            for name in ("whole", "fermi0", "fermi1", "bose0", "bose1", "mirror"):
                loads[name].wait()
        lattice = table_by_data(whole, jnp.concatenate([rb[q, k] for k in range(4)], 1))
        g = in_time(data_by_table(lattice[:64], fermi[0], fermi[1]), True)
        one, two = apart(lattice[64:])
        v = jnp.concatenate([one[:16], two[:16], one[16:], two[16:]], 0)
        v1r, v1i, v2r, v2i = in_time(data_by_table(v, bose[0], bose[1]), False)
        g1r, g1i, g2r, g2i = g
        same = jnp.where(jnp.logical_and(z == 0, o % 16 == 0), 1, 0) if q < 2 else 0
        turn = mirror[same][:, :32]
        high, low = split(jnp.concatenate(g, 1))
        turned = dot(turn, high) + dot(turn, low)
        m1r, m1i, m2r, m2i = [turned[:, 256 * k : 256 * k + 256] for k in range(4)]
        b1r, b1i = g1i * m2i - g1r * m2r, -(g1r * m2i + g1i * m2r)
        b2r, b2i = g2i * m1i - g2r * m1r, -(g2r * m1i + g2i * m1r)
        s1r, s1i = v1r * g1r - v1i * g1i, v1r * g1i + v1i * g1r
        s2r, s2i = v2r * g2r - v2i * g2i, v2r * g2i + v2i * g2r
        if q == 0:
            for name in ("fermib0", "fermib1", "boseb0", "boseb1", "wholeb"):
                loads[name].wait()
        omega = data_by_table(
            out_of_time(s1r - s2r, s1i - s2i, s1r + s2r, s1i + s2i), fermib[0], fermib[1]
        )
        nu = data_by_table(out_of_time(b1r + b2r, b1i + b2i, b1r - b2r, b1i - b2i), boseb[0], boseb[1])
        nu = together(
            jnp.concatenate([nu[:16], nu[32:48]], 0), jnp.concatenate([nu[16:32], nu[48:]], 0)
        )
        planes = table_by_data(wholeb, jnp.concatenate([omega, nu], 0))
        for k in range(4):
            tb[q, k] = planes[:, 128 * k : 128 * k + 128]
        wait_c[q] = exchange_o(planes_at(tb, q), rows_at(ub, q), other_way)

    def back(q):
        wait_c[q]()
        even, odd = [
            jnp.concatenate([ub[q, k, pl.ds(r, 16, 12), :] for r in range(8)], 0).T for k in range(2)
        ]
        pieces = []
        for r in range(4):
            one, two = [ub[q, k, pl.ds(8 + r, 16, 12), :] for k in range(2)]
            pieces.append(jnp.where(lower, one, pltpu.roll(two, 64, 1)))
            pieces.append(jnp.where(lower, pltpu.roll(one, 64, 1), two))
        both = jnp.concatenate(pieces, 0).T
        for lo in range(2):
            fermi_rows = even - odd if lo else even + odd
            bose_rows = both[:64] - both[64:] if lo else both[:64] + both[64:]
            for h in range(4):
                ta[q, 2 * h + lo, :32] = fermi_rows[32 * h : 32 * h + 32]
                ta[q, 2 * h + lo, 32:] = bose_rows[16 * h : 16 * h + 16]
        wait_d[q] = exchange_z(ta.at[q], ua.at[q])

    other_way = x_g.at[0, pl.ds(0, 372)]
    lower = lane(16, 128) < 64

    for name in ("x_g0", "x_g1", "x_v0", "x_v1"):
        loads[name].wait()
    sheet_there(x_g, x_v, sheet, loads, sa)
    pl.semaphore_wait(barrier, 38)
    for q in range(4):
        wait_a[q] = exchange_z(sa.at[q], ra.at[q])

    load("whole", whole_h.at[parity], whole)
    load("mirror", mirror_h.at[parity], mirror)
    for k in range(2):
        load("fermi" + str(k), fermi_h.at[k], fermi.at[k])
        load("bose" + str(k), bose_h.at[k], bose.at[k])
    load("wholeb", wholeb_h.at[parity], wholeb)
    for k in range(2):
        load("fermib" + str(k), fermib_h.at[k], fermib.at[k])
        load("boseb" + str(k), boseb_h.at[k], boseb.at[k])
    for k in range(2):
        load("sheetb" + str(k), sheetb_h.at[pl.ds(4 * k, 4)], sheetb.at[pl.ds(4 * k, 4)])

    there(0)
    there(1)
    middle(0)
    there(2)
    middle(1)
    there(3)
    back(0)
    middle(2)
    back(1)
    middle(3)
    back(2)
    back(3)

    loads["sheetb0"].wait()
    loads["sheetb1"].wait()
    wait_d[0]()
    wait_d[1]()
    for k, term in enumerate(sheet_back(ua, 0, sheetb)):
        half[k] = term
    wait_d[2]()
    for copy in sent:
        copy.wait_send()
    wait_d[3]()
    terms = [half[k] + term for k, term in enumerate(sheet_back(ua, 1, sheetb))]
    re, im = eight([t[:, :128] for t in terms], [t[:, 128:] for t in terms], -1)
    for p, part in enumerate((re, im)):
        for g in range(8):
            for b in range(2):
                out_g[p, pl.ds(2 * g + b, 32, 16), :] = part[g][48 * b : 48 * b + 32]
                out_v[p, pl.ds(2 * g + b, 16, 16), :] = part[g][48 * b + 32 : 48 * b + 48]


def hand_on(g, v, out_g, out_v, sem):
    ways = []
    for p in range(2):
        for half in range(2):
            ways.append([r.at[p, pl.ds(256 * half, 256)] for r in (g, out_g)])
        ways.append([r.at[p] for r in (v, out_v)])
    copies = [pltpu.make_async_copy(a, b, sem.at[k]) for k, (a, b) in enumerate(ways)]
    for copy in copies:
        copy.start()
    for copy in copies:
        copy.wait()


def view(x):
    n = x.shape[-3]
    return x.reshape(2, n, 2, 8, 128).transpose(0, 1, 3, 2, 4).reshape(2, n * 16, 128)


def unview(x):
    n = x.shape[1] // 16
    return x.reshape(2, n, 8, 2, 128).transpose(0, 1, 3, 2, 4).reshape(2, n, 2, 1024)


def per_device(green, inter):
    shapes = [
        (2, 512, 128), (2, 256, 128),
        (8, 2, 256, 256), (8, 2, 256, 256), (2, 96, 128), (2, 96, 128),
        (2, 512, 512), (2, 512, 512), (2, 256, 512), (2, 512, 256), (2, 32, 128),
        (4, 8, 48, 128), (4, 8, 48, 128), (4, 2, 192, 128), (4, 4, 96, 128),
        (4, 4, 96, 128), (4, 2, 192, 128), (4, 8, 48, 128), (4, 8, 48, 128),
        (8, 96, 256),
    ]
    scratch = [pltpu.VMEM(s, BF16 if 2 <= k < 11 else F32) for k, s in enumerate(shapes)]
    any_spec = pl.BlockSpec(memory_space=pl.ANY)
    vmem_spec = pl.BlockSpec(memory_space=pltpu.VMEM)
    constants = tables()
    out_g, out_v = pl.pallas_call(
        kernel,
        out_shape=(pltpu.VMEM((2, 512, 128), F32), pltpu.VMEM((2, 256, 128), F32)),
        in_specs=[any_spec] * (2 + len(constants)),
        out_specs=(vmem_spec, vmem_spec),
        scratch_shapes=scratch + [pltpu.SemaphoreType.DMA((n,)) for n in (26, 48)],
        compiler_params=pltpu.CompilerParams(
            collective_id=0, has_side_effects=True, vmem_limit_bytes=56 << 20
        ),
    )(view(green), view(inter), *constants)
    out_g, out_v = pl.pallas_call(
        hand_on,
        out_shape=(jax.ShapeDtypeStruct((2, 512, 128), F32), jax.ShapeDtypeStruct((2, 256, 128), F32)),
        in_specs=[vmem_spec] * 2,
        out_specs=(any_spec, any_spec),
        scratch_shapes=[pltpu.SemaphoreType.DMA((6,))],
    )(*[pltpu.with_memory_space_constraint(x, pltpu.VMEM) for x in (out_g, out_v)])
    return unview(out_g), unview(out_v)[None]


def solution(mesh):
    placed = (P(None, None, "freq", "kz", None), P(None, None, "freq", "kz", None))
    return jax.shard_map(
        per_device,
        mesh=mesh,
        in_specs=placed,
        out_specs=(P(None, "freq", "kz", None), P(None, None, "freq", "kz", None)),
        check_vma=False,
    )
```
